128 devices in a mesh: grp: 4 (over z), shard: 32 (over x, y, core).
Axes of the slice: x: 4, y: 4, z: 4, core: 2. Of those that a mesh axis runs over, the one named last changes fastest.
Arguments:
- queries: float32 [512, 1024], P(('grp', 'shard')), may hold values from -48 to 48
- cache: bfloat16 [524288, 1024], P(('grp', 'shard')), may hold values from -6 to 6
- cand_ids: int32 [512, 256], P(('grp', 'shard')), may hold values from 0 to 524287, as said below
- owner_map: int32 [4096], replicated, may hold values from 0 to 4095, as said below
- teacher_rank: int32 [512, 256], P(('grp', 'shard')), may hold values from 0 to 255, each once within a row
Outputs:
- query_grad: float32 [512, 1024], P(('grp', 'shard'))
- query_loss: float32 [512], P(('grp', 'shard'))
The draws below stay inside these ranges and needn't reach their ends.
Inputs may be any that keep to these rules, and one draw needn't show every extreme that they name: Passage p of logical block b is cache row owner_map[b] * 128 + p % 128; owner_map is a permutation, and cache rows are split evenly over the devices in mesh order. `cand_ids`: the 1024 candidates of one device's queries lie at most 16 on any one device; a quarter of the devices, the same for every requesting device, hold exactly 16 of every device's candidates.
All inputs are finite; a program needn't handle non-finite values.
Results may differ from the reference program's by a relative error of at most 0.0092.
Values may be sent and summed in bfloat16 or wider, within the bound.
A program may use at most 64 MiB of HBM per device.

```python
import math
import jax
import jax.numpy as jnp
from jax import lax

D = 1024
NC = 256
BLOCK = 128
QD = 4
NQ = 512
NB = 4096
NP = 524288
PD = 4096
DEVICES = 128


def owner_permutation(key):
    return jax.random.permutation(jax.random.fold_in(key, 101), NB).astype(jnp.int32)


def candidate_table(key):
    slot_count = QD * NC
    half_slots = slot_count // 2
    hot_count = DEVICES // 4
    cold_count = DEVICES - hot_count
    device_order = jax.random.permutation(jax.random.fold_in(key, 102), DEVICES).astype(jnp.int32)
    hot_owners = device_order[:hot_count]
    cold_owners = device_order[hot_count:]
    position = jnp.arange(half_slots, dtype=jnp.int32)

    def one_device(requester):
        device_key = jax.random.fold_in(jax.random.fold_in(key, 103), requester)
        offset_cold = jax.random.randint(jax.random.fold_in(device_key, 1), (), 0, cold_count)
        owners = jnp.concatenate([hot_owners[position % hot_count], cold_owners[(position + offset_cold) % cold_count]])
        shuffle = jax.random.permutation(jax.random.fold_in(device_key, 2), slot_count)
        owners = owners[shuffle]
        local_row = jax.random.randint(jax.random.fold_in(device_key, 3), (slot_count,), 0, PD)
        return owners * PD + local_row
    physical = jax.vmap(one_device)(jnp.arange(DEVICES, dtype=jnp.int32))
    inverse = jnp.argsort(owner_permutation(key)).astype(jnp.int32)
    logical = inverse[physical // BLOCK] * BLOCK + physical % BLOCK
    return logical.reshape(NQ, NC).astype(jnp.int32)


def cache_rows(key, row_ids):
    base_key = jax.random.fold_in(key, 104)

    def one_row(row_id):
        row_key = jax.random.fold_in(base_key, row_id)
        return jnp.clip(jax.random.normal(row_key, (D,), jnp.float32), -6.0, 6.0)
    return jax.vmap(one_row)(row_ids)


def draw_owner_map(key, part):
    return owner_permutation(key)


def draw_cand_ids(key, part):
    return candidate_table(key)


def draw_cache(key, part):
    return cache_rows(key, jnp.arange(NP, dtype=jnp.int32)).astype(jnp.bfloat16)


def draw_queries(key, part):
    query_key = jax.random.fold_in(key, 105)
    return jnp.clip(jax.random.normal(query_key, (NQ, D), jnp.float32), -6.0, 6.0)


def setup_inputs(seed: int = 0) -> dict:
    key_list = jax.random.split(jax.random.key(seed), 6)
    queries = draw_queries(jax.random.fold_in(key_list[5], 71), 0)
    cache = draw_cache(jax.random.fold_in(key_list[5], 71), 0)
    cand_ids = draw_cand_ids(jax.random.fold_in(key_list[5], 71), 0)
    owner_map = draw_owner_map(jax.random.fold_in(key_list[5], 71), 0)
    teacher_rank = jax.vmap(lambda own: jax.random.permutation(own, NC))(jax.random.split(key_list[4], NQ)).reshape((NQ, NC)).astype(jnp.int32)
    return {"queries": queries, "cache": cache, "cand_ids": cand_ids, "owner_map": owner_map, "teacher_rank": teacher_rank}


def listwise(raw_scores, teacher_rank, logit_scale):
    logits = logit_scale * raw_scores
    shifted = logits - lax.optimization_barrier(jnp.max(logits, axis=-1, keepdims=True))
    student_log = shifted - jnp.log(lax.optimization_barrier(jnp.sum(jnp.exp(shifted), axis=-1, keepdims=True)))
    teach = -teacher_rank.astype(jnp.float32) * (8.0 / teacher_rank.shape[-1])
    teach = teach - lax.optimization_barrier(jnp.max(teach, axis=-1, keepdims=True))
    teacher_log = teach - jnp.log(lax.optimization_barrier(jnp.sum(jnp.exp(teach), axis=-1, keepdims=True)))
    teacher_prob = jnp.exp(teacher_log)
    query_loss = lax.optimization_barrier(jnp.sum(teacher_prob * (teacher_log - student_log), axis=-1))
    coefficient = (jnp.exp(student_log) - teacher_prob).astype(jnp.bfloat16)
    return (query_loss, coefficient)

def reference(queries, cache, cand_ids, owner_map, teacher_rank):
    logit_scale = 3.0 / math.sqrt(D)
    physical = (jnp.take(owner_map, cand_ids // BLOCK) * BLOCK + cand_ids % BLOCK).astype(jnp.int32)
    query16 = queries.astype(jnp.bfloat16)
    group_size = 16
    blocks = NQ // group_size

    def one_block(packed):
        query_part, phys_part, rank_part = packed
        fetched = cache[phys_part].astype(jnp.float32)
        raw_scores = jnp.einsum('qd,qcd->qc', query_part.astype(jnp.float32), fetched)
        query_loss, coefficient = listwise(raw_scores, rank_part, logit_scale)
        query_grad = logit_scale * jnp.einsum('qc,qcd->qd', coefficient.astype(jnp.float32), fetched)
        return (query_grad, query_loss)
    query_grad, query_loss = lax.map(one_block, (query16.reshape(blocks, group_size, D), physical.reshape(blocks, group_size, NC), teacher_rank.reshape(blocks, group_size, NC)))
    return (query_grad.reshape(NQ, D), query_loss.reshape(NQ))
```

```python
import functools
import math

import jax
import jax.numpy as jnp
from jax import lax
from jax.experimental import pallas as pl
from jax.experimental.pallas import tpu as pltpu
from jax.sharding import PartitionSpec as P

MESH = pl.DeviceIdType.MESH
BLOCK = 128
CAP = 16
NEG = -1e30
F32 = jnp.float32
BF16 = jnp.bfloat16
I32 = jnp.int32


def iota(shape, dim):
    return lax.broadcasted_iota(I32, shape, dim)


def nt(a, b):
    return lax.dot_general(a, b, (((1,), (1,)), ((), ())), preferred_element_type=F32)


def nn(a, b):
    return jnp.dot(a, b, preferred_element_type=F32)


def hot(mask):
    return jnp.where(mask, 1.0, 0.0).astype(BF16)


def col_to_rows(col):
    eye = iota((128, 128), 0) == iota((128, 128), 1)
    rows = [
        jnp.sum(jnp.where(eye, col[k * 128 : (k + 1) * 128], 0.0), axis=0, keepdims=True)
        for k in range(col.shape[0] // 128)
    ]
    return jnp.concatenate(rows, axis=0)


def rows_to_col(rows):
    eye = iota((128, 128), 0) == iota((128, 128), 1)
    cols = [
        jnp.sum(jnp.where(eye, rows[k : k + 1], 0.0), axis=1, keepdims=True)
        for k in range(rows.shape[0])
    ]
    return jnp.concatenate(cols, axis=0)


class Dims:
    def __init__(self, n, queries, cache, cand_ids):
        self.n = n
        self.devices = 2 * n**3
        self.qd, self.width = queries
        self.held = cache[0]
        self.blocks = self.held // BLOCK
        self.cands = cand_ids[1]
        self.rows = self.devices * self.qd
        self.half = self.rows // 2
        self.part = self.half // n
        self.unit = self.part // n
        self.groups = self.devices // 8
        self.grows = 8 * self.qd
        self.stat_rows = self.rows // 128


def kernel(
    d,
    q_ref,
    cand_ref,
    map_ref,
    rank_ref,
    cache_hbm,
    grad_ref,
    loss_ref,
    c_ref,
    qall,
    qpad,
    table,
    ra,
    ra2,
    rb,
    meta,
    nbuf,
    tbuf,
    sbuf,
    cf,
    mbuf,
    dbuf,
    stat,
    sa,
    stat2,
    sb,
    pbuf,
    psend,
    rc1,
    hsend,
    rc2,
    usend,
    rc3,
    asend,
    rc4,
    cache_sem,
    q1s,
    q1r,
    q2s,
    q2r,
    q3s,
    q3r,
    q4s,
    q4r,
    tas,
    tar,
    tbs,
    tbr,
    sas,
    sar,
    sbs,
    sbr,
    r1s,
    r1r,
    r2s,
    r2r,
    r3s,
    r3r,
    r4s,
    r4r,
):
    n = d.n
    z = lax.axis_index("grp")
    shard = lax.axis_index("shard")
    x = shard // (2 * n)
    y = (shard // 2) % n
    c = shard % 2
    scale = 3.0 / math.sqrt(d.width)
    xc = x * 2 + c
    yz = y * n + z
    first = c == 0
    a = jnp.where(first, x, z)
    b = jnp.where(first, z, x)

    def dev(xx, yy, zz, cc):
        return (zz, (xx * n + yy) * 2 + cc)

    def dev_xc(j):
        return dev(j // 2, y, z, j % 2)

    def dev_yz(j):
        return dev(x, j // n, j % n, c)

    def dev_a(j):
        return dev(jnp.where(first, j, x), y, jnp.where(first, z, j), c)

    def dev_b(j):
        return dev(jnp.where(first, x, j), y, jnp.where(first, j, z), c)

    def dev_y(j):
        return dev(x, j, z, c)

    sibling = dev(x, y, z, 1 - c)
    nxc, nyz = 2 * n, n * n

    barrier = pltpu.get_barrier_semaphore()
    for delta in range(1, nxc):
        pl.semaphore_signal(barrier, inc=1, device_id=dev_xc((xc + delta) % nxc), device_id_type=MESH)
    for delta in range(1, nyz):
        pl.semaphore_signal(barrier, inc=1, device_id=dev_yz((yz + delta) % nyz), device_id_type=MESH)

    cache_copy = pltpu.make_async_copy(cache_hbm, c_ref, cache_sem)
    cache_copy.start()

    pending = []

    def send(src, dst, ssem, rsem, to):
        copy = pltpu.make_async_remote_copy(
            src_ref=src, dst_ref=dst, send_sem=ssem, recv_sem=rsem, device_id=to, device_id_type=MESH
        )
        copy.start()
        pending.append(copy)
        return copy

    q16 = q_ref[...]
    pieces = [jnp.where(a == k, q16, 0.0) for k in range(n)]
    qpad[0] = jnp.concatenate(pieces, axis=0).astype(BF16)

    teach = -rank_ref[...].astype(F32) * (8.0 / d.cands)
    teach = teach - jnp.max(teach, axis=1, keepdims=True)
    teacher_log = teach - jnp.log(jnp.sum(jnp.exp(teach), axis=1, keepdims=True))
    prob = jnp.exp(teacher_log)
    entropy = jnp.sum(prob * teacher_log, axis=1, keepdims=True)
    prob_hi = prob.astype(BF16).astype(F32)
    prob_lo = prob - prob_hi

    cand = cand_ref[...]
    blk, off = cand // BLOCK, cand % BLOCK
    omap = map_ref[...]
    map_rows = omap.shape[0]
    halves = jnp.concatenate([omap // 64, omap % 64], axis=0).astype(F32).astype(BF16)
    upper = hot(iota((d.cands, d.cands), 0) < iota((d.cands, d.cands), 1))
    total = jnp.zeros((d.devices, 1), F32)
    acc = jnp.zeros((d.devices, 128), F32)
    for i in range(d.qd):
        bi = blk[i : i + 1]
        low = hot(iota((128, d.cands), 0) == bi % 128)
        got = nn(halves, low)
        high = jnp.where(iota((map_rows, d.cands), 0) == bi // 128, 1.0, 0.0)
        pblk = (
            jnp.sum(got[:map_rows] * high, axis=0, keepdims=True) * 64.0
            + jnp.sum(got[map_rows:] * high, axis=0, keepdims=True)
        ).astype(I32)
        owner, lblk = pblk // d.blocks, pblk % d.blocks
        oz, oshard = owner // (2 * n * n), owner % (2 * n * n)
        place = ((oshard // (2 * n)) * 2 + oshard % 2) * nyz + ((oshard // 2) % n) * n + oz
        mine = jnp.where(iota((d.devices, d.cands), 0) == place, 1.0, 0.0)
        mine16 = mine.astype(BF16)
        earlier = nn(mine16, upper) + total
        pos = jnp.sum(mine * earlier, axis=0, keepdims=True).astype(I32)
        total = total + jnp.sum(mine, axis=1, keepdims=True)
        at = jnp.where(iota((CAP, d.cands), 0) == pos, 1.0, 0.0)
        planes = jnp.concatenate(
            [
                at * lblk.astype(F32),
                at * off[i : i + 1].astype(F32),
                at * float(i),
                at * prob_hi[i : i + 1],
                at * prob_lo[i : i + 1],
                jnp.zeros((128 - 5 * CAP, d.cands), F32),
            ],
            axis=0,
        ).astype(BF16)
        acc = acc + nt(mine16, planes)
    table[...] = acc

    pl.semaphore_wait(barrier, nxc - 1 + nyz - 1)

    for k in range(1, n):
        send(qpad.at[0], qpad.at[k], q1s.at[k], q1r.at[k], dev_a((a + k) % n))
    for k in range(1, nxc):
        j = (xc + k) % nxc
        send(
            table.at[pl.ds(pl.multiple_of(j * nyz, nyz), nyz)],
            ra.at[pl.ds(pl.multiple_of(xc * nyz, nyz), nyz)],
            tas.at[k],
            tar.at[k],
            dev_xc(j),
        )
    own = pl.ds(pl.multiple_of(xc * nyz, nyz), nyz)
    ra[own] = table[own]

    def arrived(dst, rsem):
        pltpu.make_async_remote_copy(
            src_ref=dst, dst_ref=dst, send_sem=rsem, recv_sem=rsem, device_id=sibling, device_id_type=MESH
        ).wait_recv()

    for k in range(1, n):
        arrived(qpad.at[k], q1r.at[k])
    unit_rows = pl.ds(pl.multiple_of(c * d.half + b * d.part + y * d.unit, d.unit), d.unit)
    gathered = qpad[0]
    for k in range(1, n):
        gathered = gathered + qpad[k]
    qall[unit_rows] = gathered
    for k in range(1, n):
        send(qall.at[unit_rows], qall.at[unit_rows], q2s.at[k], q2r.at[k], dev_y((y + k) % n))

    for k in range(1, nxc):
        src = (xc + nxc - k) % nxc
        arrived(ra.at[pl.ds(pl.multiple_of(src * nyz, nyz), nyz)], tar.at[k])
    r, s = iota((d.devices, d.devices), 0), iota((d.devices, d.devices), 1)
    perm = hot((r % nxc) * nyz + r // nxc == s)
    ra2[...] = nn(perm, ra[...].astype(BF16))
    for k in range(1, nyz):
        j = (yz + k) % nyz
        send(
            ra2.at[pl.ds(pl.multiple_of(j * nxc, nxc), nxc)],
            rb.at[pl.ds(pl.multiple_of(yz * nxc, nxc), nxc)],
            tbs.at[k],
            tbr.at[k],
            dev_yz(j),
        )
    own = pl.ds(pl.multiple_of(yz * nxc, nxc), nxc)
    rb[own] = ra2[own]

    for k in range(1, n):
        src = (y + n - k) % n
        rows = pl.ds(pl.multiple_of(c * d.half + b * d.part + src * d.unit, d.unit), d.unit)
        arrived(qall.at[rows], q2r.at[k])
    part_rows = pl.ds(pl.multiple_of(c * d.half + b * d.part, d.part), d.part)
    for k in range(1, n):
        send(qall.at[part_rows], qall.at[part_rows], q3s.at[k], q3r.at[k], dev_b((b + k) % n))

    for k in range(1, nyz):
        src = (yz + nyz - k) % nyz
        arrived(rb.at[pl.ds(pl.multiple_of(src * nxc, nxc), nxc)], tbr.at[k])
    pc, pb, py, pa = r // n**3, (r // n**2) % n, (r // n) % n, r % n
    px, pz = jnp.where(pc == 0, pa, pb), jnp.where(pc == 0, pb, pa)
    perm = hot(((py * n + pz) * n + px) * 2 + pc == s)
    lists = nn(perm, rb[...].astype(BF16)).astype(BF16)
    lane = iota((128, 128), 1)
    sub = iota((128, 128), 0)
    pick = jnp.where(iota((d.devices, 128), 0) % 8 == iota((d.devices, 128), 1) // CAP, 1.0, 0.0)
    for p in range(5):
        spread = nn(lists, hot(sub == p * CAP + lane % CAP)) * pick
        meta[p] = jnp.sum(spread.reshape(d.groups, 8, 128), axis=1)

    def fill(g, _):
        lb, lo, lq, hi, low = [meta[p, pl.ds(g, 1), :] for p in range(5)]
        key = lb.astype(I32) * d.grows + (iota((1, 128), 1) // CAP) * d.qd + lq.astype(I32)
        same = iota((128, 128), 0) == lo.astype(I32)
        zero = jnp.zeros((128, 128), F32)
        right = jnp.concatenate(
            [
                jnp.concatenate([jnp.where(same & (hi > 0.0), 1.0, 0.0), zero], axis=1),
                jnp.concatenate([jnp.where(same, hi, 0.0), jnp.where(same, low, 0.0)], axis=1),
            ],
            axis=0,
        ).astype(BF16)
        step = max(1, 256 // d.grows)
        for c0 in range(0, d.blocks, step):
            left = hot(iota((step * d.grows, 128), 0) + c0 * d.grows == key)
            out = nt(jnp.concatenate([left, left], axis=1), right)
            rows = pl.ds(pl.multiple_of(g * d.grows, d.grows), d.grows)
            for k in range(step):
                cols = slice((c0 + k) * 128, (c0 + k + 1) * 128)
                nbuf[rows, cols] = out[k * d.grows : (k + 1) * d.grows, :128]
                tbuf[rows, cols] = out[k * d.grows : (k + 1) * d.grows, 128:]
        return 0

    lax.fori_loop(0, d.groups, fill, 0)

    for k in range(1, n):
        src = (b + n - k) % n
        rows = pl.ds(pl.multiple_of(c * d.half + src * d.part, d.part), d.part)
        arrived(qall.at[rows], q3r.at[k])
    half_rows = pl.ds(pl.multiple_of(c * d.half, d.half), d.half)
    other_rows = pl.ds(pl.multiple_of((1 - c) * d.half, d.half), d.half)
    send(qall.at[half_rows], qall.at[half_rows], q4s.at[0], q4r.at[0], sibling)
    cache_copy.wait()
    arrived(qall.at[other_rows], q4r.at[0])

    mbuf[...] = jnp.full(mbuf.shape, NEG, F32)
    dbuf[...] = jnp.zeros(dbuf.shape, F32)
    tile = 256

    def score(t, _):
        cols = pl.ds(pl.multiple_of(t * tile, tile), tile)
        logits = nt(qall[...], c_ref[cols, :]) * scale
        dd = tbuf[:, cols] * logits
        logits = jnp.where(nbuf[:, cols] > 0.0, logits, NEG)
        sbuf[:, cols] = logits
        mbuf[...] = jnp.maximum(mbuf[...], jnp.maximum(logits[:, :128], logits[:, 128:]))
        dbuf[...] += dd[:, :128] + dd[:, 128:]
        return 0

    lax.fori_loop(0, d.held // tile, score, 0)
    top = jnp.max(mbuf[...], axis=1, keepdims=True)
    dot_t = jnp.sum(dbuf[...], axis=1, keepdims=True)
    dbuf[...] = jnp.zeros(dbuf.shape, F32)
    mbuf[...] = jnp.broadcast_to(top, mbuf.shape)

    def expo(t, _):
        cols = pl.ds(pl.multiple_of(t * 128, 128), 128)
        e = nbuf[:, cols] * jnp.exp(sbuf[:, cols] - mbuf[...])
        sbuf[:, cols] = e
        dbuf[...] += e
        return 0

    lax.fori_loop(0, d.held // 128, expo, 0)
    total = jnp.sum(dbuf[...], axis=1, keepdims=True)

    nr = d.stat_rows
    my_top = col_to_rows(top)
    packed = [my_top, col_to_rows(total), col_to_rows(dot_t)]
    if 16 - 3 * nr:
        packed.append(jnp.zeros((16 - 3 * nr, 128), F32))
    stat[...] = jnp.concatenate(packed, axis=0)

    def combine(pieces):
        tops = [p[:nr] for p in pieces]
        best = functools.reduce(jnp.maximum, tops)
        zs = sum(p[nr : 2 * nr] * jnp.exp(t - best) for p, t in zip(pieces, tops))
        ds = sum(p[2 * nr : 3 * nr] for p in pieces)
        return best, zs, ds

    for k in range(1, nxc):
        send(stat, sa.at[k], sas.at[k], sar.at[k], dev_xc((xc + k) % nxc))
    for k in range(1, nxc):
        arrived(sa.at[k], sar.at[k])
    packed = list(combine([stat[...]] + [sa[k] for k in range(1, nxc)]))
    if 16 - 3 * nr:
        packed.append(jnp.zeros((16 - 3 * nr, 128), F32))
    stat2[...] = jnp.concatenate(packed, axis=0)
    for k in range(1, nyz):
        send(stat2, sb.at[k], sbs.at[k], sbr.at[k], dev_yz((yz + k) % nyz))
    for k in range(1, nyz):
        arrived(sb.at[k], sbr.at[k])
    best, zs, ds = combine([stat2[...]] + [sb[k] for k in range(1, nyz)])

    losses = best + jnp.log(zs) - ds
    flat = iota((nr, 128), 0) * 128 + iota((nr, 128), 1)
    row0 = c * d.half + b * d.part + y * d.unit + a * d.qd
    out = jnp.zeros((1, 128), F32)
    for i in range(d.qd):
        value = jnp.sum(
            jnp.sum(jnp.where(flat == row0 + i, losses, 0.0), axis=0, keepdims=True), axis=1, keepdims=True
        )
        out = jnp.where(iota((1, 128), 1) == i, value + entropy[i : i + 1], out)
    loss_ref[...] = out[:, : d.qd]

    mbuf[...] = jnp.broadcast_to(rows_to_col(jnp.exp(my_top - best) / zs), mbuf.shape)

    def coef(t, _):
        cols = pl.ds(pl.multiple_of(t * 128, 128), 128)
        cf[:, cols] = (sbuf[:, cols] * mbuf[...] - tbuf[:, cols]).astype(BF16)
        return 0

    lax.fori_loop(0, d.held // 128, coef, 0)

    for t in range(d.width // 256):
        cols = slice(t * 256, (t + 1) * 256)
        got = nn(cf[...], c_ref[:, cols]) * scale
        pbuf[:, cols] = got
        psend[:, cols] = got.astype(BF16)

    send(psend.at[other_rows], rc1, r1s.at[0], r1r.at[0], sibling)
    arrived(rc1, r1r.at[0])
    pbuf[half_rows] = pbuf[half_rows] + rc1[...].astype(F32)
    hsend[...] = pbuf[half_rows].astype(BF16)
    for k in range(1, n):
        j = (b + k) % n
        send(
            hsend.at[pl.ds(pl.multiple_of(j * d.part, d.part), d.part)],
            rc2.at[k],
            r2s.at[k],
            r2r.at[k],
            dev_b(j),
        )
    for k in range(1, n):
        arrived(rc2.at[k], r2r.at[k])
    part = pbuf[part_rows]
    for k in range(1, n):
        part = part + rc2[k].astype(F32)
    pbuf[part_rows] = part
    usend[...] = part.astype(BF16)
    for k in range(1, n):
        j = (y + k) % n
        send(
            usend.at[pl.ds(pl.multiple_of(j * d.unit, d.unit), d.unit)],
            rc3.at[k],
            r3s.at[k],
            r3r.at[k],
            dev_y(j),
        )
    for k in range(1, n):
        arrived(rc3.at[k], r3r.at[k])
    unit = pbuf[unit_rows]
    for k in range(1, n):
        unit = unit + rc3[k].astype(F32)
    for k in range(n):
        asend[k, : d.qd] = unit[k * d.qd : (k + 1) * d.qd]
    for k in range(1, n):
        j = (a + k) % n
        send(asend.at[j], rc4.at[k], r4s.at[k], r4r.at[k], dev_a(j))
    mine = asend[a]
    for k in range(1, n):
        arrived(rc4.at[k], r4r.at[k])
    for k in range(1, n):
        mine = mine + rc4[k]
    grad_ref[...] = mine[: d.qd]

    for copy in pending:
        copy.wait_send()


def per_device(n, queries, cache, cand_ids, owner_map, teacher_rank):
    d = Dims(n, queries.shape, cache.shape, cand_ids.shape)
    w = d.width
    nxc, nyz = 2 * n, n * n
    dma = lambda k: [pltpu.SemaphoreType.DMA((k,))] * 2
    vmem = pl.BlockSpec(memory_space=pltpu.VMEM)
    grad, loss = pl.pallas_call(
        functools.partial(kernel, d),
        out_shape=(
            jax.ShapeDtypeStruct((d.qd, w), F32),
            jax.ShapeDtypeStruct((1, d.qd), F32),
        ),
        in_specs=[vmem] * 4 + [pl.BlockSpec(memory_space=pl.ANY)],
        out_specs=(vmem, vmem),
        scratch_shapes=[
            pltpu.VMEM((d.held, w), BF16),
            pltpu.VMEM((d.rows, w), BF16),
            pltpu.VMEM((n, d.unit, w), BF16),
            pltpu.VMEM((d.devices, 128), F32),
            pltpu.VMEM((d.devices, 128), F32),
            pltpu.VMEM((d.devices, 128), F32),
            pltpu.VMEM((d.devices, 128), F32),
            pltpu.VMEM((5, d.groups, 128), F32),
            pltpu.VMEM((d.rows, d.held), F32),
            pltpu.VMEM((d.rows, d.held), F32),
            pltpu.VMEM((d.rows, d.held), F32),
            pltpu.VMEM((d.rows, d.held), BF16),
            pltpu.VMEM((d.rows, 128), F32),
            pltpu.VMEM((d.rows, 128), F32),
            pltpu.VMEM((16, 128), F32),
            pltpu.VMEM((nxc, 16, 128), F32),
            pltpu.VMEM((16, 128), F32),
            pltpu.VMEM((nyz, 16, 128), F32),
            pltpu.VMEM((d.rows, w), F32),
            pltpu.VMEM((d.rows, w), BF16),
            pltpu.VMEM((d.half, w), BF16),
            pltpu.VMEM((d.half, w), BF16),
            pltpu.VMEM((n, d.part, w), BF16),
            pltpu.VMEM((d.part, w), BF16),
            pltpu.VMEM((n, d.unit, w), BF16),
            pltpu.VMEM((n, 8, w), F32),
            pltpu.VMEM((n, 8, w), F32),
            pltpu.SemaphoreType.DMA,
            *dma(n),
            *dma(n),
            *dma(n),
            *dma(1),
            *dma(nxc),
            *dma(nyz),
            *dma(nxc),
            *dma(nyz),
            *dma(1),
            *dma(n),
            *dma(n),
            *dma(n),
        ],
        compiler_params=pltpu.CompilerParams(
            collective_id=0, has_side_effects=True, vmem_limit_bytes=58 * 2**20
        ),
    )(queries, cand_ids, owner_map.reshape(-1, 128), teacher_rank, cache)
    return grad, loss.reshape(d.qd)


def solution(mesh):
    n = mesh.shape["grp"]
    both = P(("grp", "shard"), None)
    return jax.shard_map(
        functools.partial(per_device, n),
        mesh=mesh,
        in_specs=(both, both, both, P(), both),
        out_specs=(both, P(("grp", "shard"))),
        check_vma=False,
    )
```

```python
import functools
import math

import jax
import jax.numpy as jnp
from jax import lax
from jax.experimental import pallas as pl
from jax.experimental.pallas import tpu as pltpu
from jax.sharding import PartitionSpec as P

MESH = pl.DeviceIdType.MESH
BLOCK = 128
CAP = 16
CUTS = 2
NEG = -1e30
F32 = jnp.float32
BF16 = jnp.bfloat16
I32 = jnp.int32


def iota(shape, dim):
    return lax.broadcasted_iota(I32, shape, dim)


def nt(a, b):
    return lax.dot_general(a, b, (((1,), (1,)), ((), ())), preferred_element_type=F32)


def nn(a, b):
    return jnp.dot(a, b, preferred_element_type=F32)


def hot(mask):
    return jnp.where(mask, 1.0, 0.0).astype(BF16)


def col_to_rows(col):
    eye = iota((128, 128), 0) == iota((128, 128), 1)
    rows = [
        jnp.sum(jnp.where(eye, col[k * 128 : (k + 1) * 128], 0.0), axis=0, keepdims=True)
        for k in range(col.shape[0] // 128)
    ]
    return jnp.concatenate(rows, axis=0)


def rows_to_col(rows):
    eye = iota((128, 128), 0) == iota((128, 128), 1)
    cols = [
        jnp.sum(jnp.where(eye, rows[k : k + 1], 0.0), axis=1, keepdims=True)
        for k in range(rows.shape[0])
    ]
    return jnp.concatenate(cols, axis=0)


class Dims:
    def __init__(self, n, queries, cache, cand_ids):
        self.n = n
        self.chips = n**3
        self.devices = 2 * self.chips
        self.qd, self.width = queries
        self.held = cache[0]
        self.blocks = self.held // BLOCK
        self.cands = cand_ids[1]
        self.rows = self.devices * self.qd
        self.half = self.rows // 2
        self.groups = self.devices // 8
        self.grows = 8 * self.qd
        self.stat_rows = self.rows // 128
        self.layer = n * n
        self.tile = min(1024, self.held)
        self.cut = self.width // CUTS


def kernel(
    d,
    q_ref,
    cand_ref,
    map_ref,
    rank_ref,
    cache_hbm,
    grad_ref,
    loss_ref,
    c_ref,
    qown,
    qrecv,
    qall,
    table,
    ra,
    ra2,
    rb,
    meta,
    nbuf,
    tbuf,
    sbuf,
    et,
    mbuf,
    zbuf,
    dbuf,
    stat,
    sa,
    stat2,
    sb,
    uv,
    csend,
    crecv,
    psend,
    precv,
    cache_sem,
    qs,
    qr,
    xs,
    xr,
    tas,
    tar,
    tbs,
    tbr,
    sas,
    sar,
    sbs,
    sbr,
    cs,
    cr,
    ps,
    pr,
):
    n = d.n
    z = lax.axis_index("grp")
    shard = lax.axis_index("shard")
    x = shard // (2 * n)
    y = (shard // 2) % n
    c = shard % 2
    scale = 3.0 / math.sqrt(d.width)
    xc = x * 2 + c
    yz = y * n + z
    chip = z * d.layer + shard // 2
    nxc, nyz = 2 * n, n * n

    def dev(xx, yy, zz, cc):
        return (zz, (xx * n + yy) * 2 + cc)

    def dev_xc(j):
        return dev(j // 2, y, z, j % 2)

    def dev_yz(j):
        return dev(x, j // n, j % n, c)

    def dev_chip(h):
        return (h // d.layer, (h % d.layer) * 2 + c)

    sibling = dev(x, y, z, 1 - c)

    barrier = pltpu.get_barrier_semaphore()

    def greet(k, _):
        pl.semaphore_signal(
            barrier, inc=1, device_id=dev_chip((chip + k) % d.chips), device_id_type=MESH
        )
        return 0

    lax.fori_loop(1, d.chips, greet, 0)
    other_core = 0
    for k in range(1, nxc):
        if k % 2:
            other_core += 1
            pl.semaphore_signal(barrier, inc=1, device_id=dev_xc((xc + k) % nxc), device_id_type=MESH)

    cache_copy = pltpu.make_async_copy(cache_hbm, c_ref, cache_sem)
    cache_copy.start()

    pending = []

    def remote(src, dst, ssem, rsem, to):
        return pltpu.make_async_remote_copy(
            src_ref=src, dst_ref=dst, send_sem=ssem, recv_sem=rsem, device_id=to, device_id_type=MESH
        )

    def send(src, dst, ssem, rsem, to):
        copy = remote(src, dst, ssem, rsem, to)
        copy.start()
        pending.append(copy)

    def arrived(dst, rsem):
        remote(dst, dst, rsem, rsem, sibling).wait_recv()

    def sent(src, ssem):
        remote(src, src, ssem, ssem, sibling).wait_send()

    q16 = q_ref[...].astype(BF16)
    qown[...] = q16
    qrecv[chip] = q16

    teach = -rank_ref[...].astype(F32) * (8.0 / d.cands)
    teach = teach - jnp.max(teach, axis=1, keepdims=True)
    teacher_log = teach - jnp.log(jnp.sum(jnp.exp(teach), axis=1, keepdims=True))
    prob = jnp.exp(teacher_log)
    entropy = jnp.sum(prob * teacher_log, axis=1, keepdims=True)
    prob_hi = prob.astype(BF16).astype(F32)
    prob_lo = prob - prob_hi

    cand = cand_ref[...]
    blk, off = cand // BLOCK, cand % BLOCK
    omap = map_ref[...]
    map_rows = omap.shape[0]
    halves = jnp.concatenate([omap // 64, omap % 64], axis=0).astype(F32).astype(BF16)
    upper = hot(iota((d.cands, d.cands), 0) < iota((d.cands, d.cands), 1))
    total = jnp.zeros((d.devices, 1), F32)
    acc = jnp.zeros((d.devices, 128), F32)
    for i in range(d.qd):
        bi = blk[i : i + 1]
        low = hot(iota((128, d.cands), 0) == bi % 128)
        got = nn(halves, low)
        high = jnp.where(iota((map_rows, d.cands), 0) == bi // 128, 1.0, 0.0)
        pblk = (
            jnp.sum(got[:map_rows] * high, axis=0, keepdims=True) * 64.0
            + jnp.sum(got[map_rows:] * high, axis=0, keepdims=True)
        ).astype(I32)
        owner, lblk = pblk // d.blocks, pblk % d.blocks
        oz, oshard = owner // (2 * n * n), owner % (2 * n * n)
        place = ((oshard // (2 * n)) * 2 + oshard % 2) * nyz + ((oshard // 2) % n) * n + oz
        mine = jnp.where(iota((d.devices, d.cands), 0) == place, 1.0, 0.0)
        mine16 = mine.astype(BF16)
        earlier = nn(mine16, upper) + total
        pos = jnp.sum(mine * earlier, axis=0, keepdims=True).astype(I32)
        total = total + jnp.sum(mine, axis=1, keepdims=True)
        at = jnp.where(iota((CAP, d.cands), 0) == pos, 1.0, 0.0)
        planes = jnp.concatenate(
            [
                at * lblk.astype(F32),
                at * off[i : i + 1].astype(F32),
                at * float(i),
                at * prob_hi[i : i + 1],
                at * prob_lo[i : i + 1],
                jnp.zeros((128 - 5 * CAP, d.cands), F32),
            ],
            axis=0,
        ).astype(BF16)
        acc = acc + nt(mine16, planes)
    table[...] = acc

    pl.semaphore_wait(barrier, d.chips - 1 + other_core)

    for k in range(1, nxc):
        j = (xc + k) % nxc
        send(
            table.at[pl.ds(pl.multiple_of(j * nyz, nyz), nyz)],
            ra.at[pl.ds(pl.multiple_of(xc * nyz, nyz), nyz)],
            tas.at[k],
            tar.at[k],
            dev_xc(j),
        )

    def give(k, _):
        remote(qown, qrecv.at[chip], qs.at[0], qr.at[z], dev_chip((chip + k) % d.chips)).start()
        return 0

    lax.fori_loop(1, d.chips, give, 0)
    own = pl.ds(pl.multiple_of(xc * nyz, nyz), nyz)
    ra[own] = table[own]
    for k in range(1, nxc):
        src = (xc + nxc - k) % nxc
        arrived(ra.at[pl.ds(pl.multiple_of(src * nyz, nyz), nyz)], tar.at[k])

    r, s = iota((d.devices, d.devices), 0), iota((d.devices, d.devices), 1)
    perm = hot((r % nxc) * nyz + r // nxc == s)
    ra2[...] = nn(perm, ra[...].astype(BF16))
    for k in range(1, nyz):
        j = (yz + k) % nyz
        send(
            ra2.at[pl.ds(pl.multiple_of(j * nxc, nxc), nxc)],
            rb.at[pl.ds(pl.multiple_of(yz * nxc, nxc), nxc)],
            tbs.at[k],
            tbr.at[k],
            dev_yz(j),
        )
    own = pl.ds(pl.multiple_of(yz * nxc, nxc), nxc)
    rb[own] = ra2[own]
    for k in range(1, nyz):
        src = (yz + nyz - k) % nyz
        arrived(rb.at[pl.ds(pl.multiple_of(src * nxc, nxc), nxc)], tbr.at[k])

    rc = jnp.where(r < d.chips, c, 1 - c)
    rh = r % d.chips
    rz, rx, ry = rh // d.layer, (rh // n) % n, rh % n
    perm = hot(((ry * n + rz) * n + rx) * 2 + rc == s)
    lists = nn(perm, rb[...].astype(BF16)).astype(BF16)
    lane = iota((128, 128), 1)
    sub = iota((128, 128), 0)
    pick = jnp.where(iota((d.devices, 128), 0) % 8 == iota((d.devices, 128), 1) // CAP, 1.0, 0.0)
    for p in range(5):
        spread = nn(lists, hot(sub == p * CAP + lane % CAP)) * pick
        meta[p] = jnp.sum(spread.reshape(d.groups, 8, 128), axis=1)

    def fill(g, _):
        lb, lo, lq, hi, low = [meta[p, pl.ds(g, 1), :] for p in range(5)]
        key = lb.astype(I32) * d.grows + (iota((1, 128), 1) // CAP) * d.qd + lq.astype(I32)
        same = iota((128, 128), 0) == lo.astype(I32)
        zero = jnp.zeros((128, 128), F32)
        right = jnp.concatenate(
            [
                jnp.concatenate([jnp.where(same & (hi > 0.0), 1.0, 0.0), zero], axis=1),
                jnp.concatenate([jnp.where(same, hi, 0.0), jnp.where(same, low, 0.0)], axis=1),
            ],
            axis=0,
        ).astype(BF16)
        step = max(1, 256 // d.grows)
        for c0 in range(0, d.blocks, step):
            left = hot(iota((step * d.grows, 128), 0) + c0 * d.grows == key)
            out = nt(jnp.concatenate([left, left], axis=1), right)
            rows = pl.ds(pl.multiple_of(g * d.grows, d.grows), d.grows)
            for k in range(step):
                cols = slice((c0 + k) * 128, (c0 + k + 1) * 128)
                nbuf[rows, cols] = out[k * d.grows : (k + 1) * d.grows, :128]
                tp = out[k * d.grows : (k + 1) * d.grows, 128:]
                tbuf[rows, cols] = tp
                et[pl.ds(pl.multiple_of(d.rows + g * d.grows, d.grows), d.grows), cols] = tp.astype(BF16)
        return 0

    lax.fori_loop(0, d.groups, fill, 0)

    per = max(1, 16 // d.qd)
    for k in range(n):
        layer = (z + k) % n
        count = d.layer - 1 if k == 0 else d.layer
        arrived(qrecv.at[pl.ds(layer * d.layer, count)], qr.at[layer])
        for i in range(0, d.layer, per):
            rows = [qrecv[layer * d.layer + i + j].astype(F32) for j in range(per)]
            at = pl.multiple_of((layer * d.layer + i) * d.qd, per * d.qd)
            qall[pl.ds(at, per * d.qd)] = jnp.concatenate(rows, axis=0).astype(BF16)
        size = d.layer * d.qd
        here = pl.ds(pl.multiple_of(layer * size, size), size)
        there = pl.ds(pl.multiple_of(d.half + layer * size, size), size)
        send(qall.at[here], qall.at[there], xs.at[k], xr.at[layer], sibling)
    cache_copy.wait()
    cache_waited = True

    mbuf[...] = jnp.full(mbuf.shape, NEG, F32)
    zbuf[...] = jnp.zeros(zbuf.shape, F32)
    dbuf[...] = jnp.zeros(dbuf.shape, F32)
    halves = [slice(0, d.half), slice(d.half, d.rows)]

    def score(rows, cols):
        raw = nt(qall[rows], c_ref[cols, :])
        raw = jnp.where(nbuf[rows, cols] > 0.0, raw, NEG)
        sbuf[rows, cols] = raw
        best = mbuf[rows]
        for k in range(d.tile // 128):
            best = jnp.maximum(best, raw[:, k * 128 : (k + 1) * 128])
        mbuf[rows] = best

    def expo(rows, t):
        step = min(64, d.half)
        for r0 in range(rows.start, rows.stop, step):
            rr = slice(r0, r0 + step)
            top = mbuf[rr]
            za, da = zbuf[rr], dbuf[rr]
            for k in range(d.tile // 128):
                cols = pl.ds(pl.multiple_of(t * d.tile + k * 128, 128), 128)
                raw = sbuf[rr, cols]
                e = nbuf[rr, cols] * jnp.exp((raw - top) * scale)
                et[rr, cols] = e.astype(BF16)
                za = za + e
                da = da + tbuf[rr, cols] * raw
            zbuf[rr], dbuf[rr] = za, da

    def widest(rows):
        mbuf[rows] = jnp.broadcast_to(jnp.max(mbuf[rows], axis=1, keepdims=True), (d.half, 128))

    def tiles(body):
        def step(t, _):
            body(t, pl.ds(pl.multiple_of(t * d.tile, d.tile), d.tile))
            return 0

        lax.fori_loop(0, d.held // d.tile, step, 0)

    tiles(lambda t, cols: score(halves[0], cols))
    widest(halves[0])
    for layer in range(n):
        size = d.layer * d.qd
        arrived(qall.at[pl.ds(d.half + layer * size, size)], xr.at[layer])

    def both(t, cols):
        score(halves[1], cols)
        expo(halves[0], t)

    tiles(both)
    widest(halves[1])
    tiles(lambda t, cols: expo(halves[1], t))

    nr = d.stat_rows
    my_top = col_to_rows(mbuf[:, :1]) * scale
    packed = [
        my_top,
        col_to_rows(jnp.sum(zbuf[...], axis=1, keepdims=True)),
        col_to_rows(jnp.sum(dbuf[...], axis=1, keepdims=True)) * scale,
    ]
    spare = [jnp.zeros((16 - 3 * nr, 128), F32)] if 16 - 3 * nr else []
    stat[...] = jnp.concatenate(packed + spare, axis=0)

    def swap(v):
        return jnp.concatenate([v[nr // 2 :], v[: nr // 2]], axis=0)

    def combine(pieces):
        tops = [p[0] for p in pieces]
        best = functools.reduce(jnp.maximum, tops)
        zs = sum(p[1] * jnp.exp(t - best) for p, t in zip(pieces, tops))
        ds = sum(p[2] for p in pieces)
        return best, zs, ds

    def three(v):
        return [v[:nr], v[nr : 2 * nr], v[2 * nr : 3 * nr]]

    for k in range(1, nxc):
        send(stat, sa.at[k], sas.at[k], sar.at[k], dev_xc((xc + k) % nxc))

    uv_cols = 256

    def product(t, _):
        cols = pl.ds(pl.multiple_of(t * uv_cols, uv_cols), uv_cols)
        uv[:, cols] = nn(et[...], c_ref[:, cols])
        return 0

    steps = d.width // uv_cols
    lax.fori_loop(0, steps // 2, product, 0)
    for k in range(1, nxc):
        arrived(sa.at[k], sar.at[k])
    pieces = [three(stat[...])]
    for k in range(1, nxc):
        got = three(sa[k])
        pieces.append([swap(v) for v in got] if k % 2 else got)
    stat2[...] = jnp.concatenate(list(combine(pieces)) + spare, axis=0)
    for k in range(1, nyz):
        send(stat2, sb.at[k], sbs.at[k], sbr.at[k], dev_yz((yz + k) % nyz))
    lax.fori_loop(steps // 2, steps, product, 0)
    for k in range(1, nyz):
        arrived(sb.at[k], sbr.at[k])
    best, zs, ds = combine([three(stat2[...])] + [three(sb[k]) for k in range(1, nyz)])

    zbuf[...] = jnp.broadcast_to(rows_to_col(scale * jnp.exp(my_top - best) / zs), zbuf.shape)

    def part(rows, cols):
        wide = jnp.concatenate([zbuf[rows]] * (d.cut // 128), axis=1)
        return uv[rows, cols] * wide - uv[slice(d.rows + rows.start, d.rows + rows.stop), cols] * scale

    cuts = [slice(i * d.cut, (i + 1) * d.cut) for i in range(CUTS)]
    for i in range(CUTS):
        csend[i] = part(halves[1], cuts[i]).astype(BF16)
        send(csend.at[i], crecv.at[i], cs.at[i], cr.at[i], sibling)

    for i in range(CUTS):
        mine = part(halves[0], cuts[i])
        arrived(crecv.at[i], cr.at[i])
        mine = (mine + crecv[i].astype(F32)).astype(BF16).astype(F32)
        for h in range(d.chips):
            psend[i, h] = mine[h * d.qd : (h + 1) * d.qd].astype(BF16)
        precv[i, chip] = psend[i, chip]

        def give_back(k, _, i=i):
            h = (chip + k) % d.chips
            remote(psend.at[i, h], precv.at[i, chip], ps.at[i], pr.at[i], dev_chip(h)).start()
            return 0

        lax.fori_loop(1, d.chips, give_back, 0)

    losses = best + jnp.log(zs) - ds
    flat = iota((nr, 128), 0) * 128 + iota((nr, 128), 1)
    out = jnp.zeros((1, 128), F32)
    for i in range(d.qd):
        value = jnp.sum(
            jnp.sum(jnp.where(flat == chip * d.qd + i, losses, 0.0), axis=0, keepdims=True),
            axis=1,
            keepdims=True,
        )
        out = jnp.where(iota((1, 128), 1) == i, value + entropy[i : i + 1], out)
    loss_ref[...] = out[:, : d.qd]

    for i in range(CUTS):
        arrived(precv.at[i, pl.ds(0, d.chips - 1)], pr.at[i])
        total = precv[i, 0].astype(F32)
        for h in range(1, d.chips):
            total = total + precv[i, h].astype(F32)
        grad_ref[:, cuts[i]] = total

    for copy in pending:
        copy.wait_send()
    sent(qrecv.at[pl.ds(0, d.chips - 1)], qs.at[0])
    for i in range(CUTS):
        sent(psend.at[i, pl.ds(0, d.chips - 1)], ps.at[i])


def per_device(n, queries, cache, cand_ids, owner_map, teacher_rank):
    d = Dims(n, queries.shape, cache.shape, cand_ids.shape)
    w = d.width
    nxc, nyz = 2 * n, n * n
    dma = lambda k: [pltpu.SemaphoreType.DMA((k,))] * 2
    vmem = pl.BlockSpec(memory_space=pltpu.VMEM)
    grad, loss = pl.pallas_call(
        functools.partial(kernel, d),
        out_shape=(
            jax.ShapeDtypeStruct((d.qd, w), F32),
            jax.ShapeDtypeStruct((1, d.qd), F32),
        ),
        in_specs=[vmem] * 4 + [pl.BlockSpec(memory_space=pl.ANY)],
        out_specs=(vmem, vmem),
        scratch_shapes=[
            pltpu.VMEM((d.held, w), BF16),
            pltpu.VMEM((d.qd, w), BF16),
            pltpu.VMEM((d.chips, d.qd, w), BF16),
            pltpu.VMEM((d.rows, w), BF16),
            pltpu.VMEM((d.devices, 128), F32),
            pltpu.VMEM((d.devices, 128), F32),
            pltpu.VMEM((d.devices, 128), F32),
            pltpu.VMEM((d.devices, 128), F32),
            pltpu.VMEM((5, d.groups, 128), F32),
            pltpu.VMEM((d.rows, d.held), F32),
            pltpu.VMEM((d.rows, d.held), F32),
            pltpu.VMEM((d.rows, d.held), F32),
            pltpu.VMEM((2 * d.rows, d.held), BF16),
            pltpu.VMEM((d.rows, 128), F32),
            pltpu.VMEM((d.rows, 128), F32),
            pltpu.VMEM((d.rows, 128), F32),
            pltpu.VMEM((16, 128), F32),
            pltpu.VMEM((nxc, 16, 128), F32),
            pltpu.VMEM((16, 128), F32),
            pltpu.VMEM((nyz, 16, 128), F32),
            pltpu.VMEM((2 * d.rows, w), F32),
            pltpu.VMEM((CUTS, d.half, d.cut), BF16),
            pltpu.VMEM((CUTS, d.half, d.cut), BF16),
            pltpu.VMEM((CUTS, d.chips, d.qd, d.cut), BF16),
            pltpu.VMEM((CUTS, d.chips, d.qd, d.cut), BF16),
            pltpu.SemaphoreType.DMA,
            pltpu.SemaphoreType.DMA((1,)),
            pltpu.SemaphoreType.DMA((n,)),
            *dma(n),
            *dma(nxc),
            *dma(nyz),
            *dma(nxc),
            *dma(nyz),
            *dma(CUTS),
            *dma(CUTS),
        ],
        compiler_params=pltpu.CompilerParams(
            collective_id=0, has_side_effects=True, vmem_limit_bytes=60 * 2**20
        ),
    )(queries, cand_ids, owner_map.reshape(-1, 128), teacher_rank, cache)
    return grad, loss.reshape(d.qd)


def solution(mesh):
    n = mesh.shape["grp"]
    both = P(("grp", "shard"), None)
    return jax.shard_map(
        functools.partial(per_device, n),
        mesh=mesh,
        in_specs=(both, both, both, P(), both),
        out_specs=(both, P(("grp", "shard"))),
        check_vma=False,
    )
```

```python
import functools
import math

import jax
import jax.numpy as jnp
from jax import lax
from jax.experimental import pallas as pl
from jax.experimental.pallas import tpu as pltpu
from jax.sharding import PartitionSpec as P

MESH = pl.DeviceIdType.MESH
BLOCK = 128
CAP = 16
CUTS = 2
NEG = -1e30
F32 = jnp.float32
BF16 = jnp.bfloat16
I32 = jnp.int32


def iota(shape, dim):
    return lax.broadcasted_iota(I32, shape, dim)


def nt(a, b):
    return lax.dot_general(a, b, (((1,), (1,)), ((), ())), preferred_element_type=F32)


def nn(a, b):
    return jnp.dot(a, b, preferred_element_type=F32)


def hot(mask):
    return jnp.where(mask, 1.0, 0.0).astype(BF16)


def col_to_rows(col):
    eye = iota((128, 128), 0) == iota((128, 128), 1)
    rows = [
        jnp.sum(jnp.where(eye, col[k * 128 : (k + 1) * 128], 0.0), axis=0, keepdims=True)
        for k in range(col.shape[0] // 128)
    ]
    return jnp.concatenate(rows, axis=0)


def rows_to_col(rows):
    eye = iota((128, 128), 0) == iota((128, 128), 1)
    cols = [
        jnp.sum(jnp.where(eye, rows[k : k + 1], 0.0), axis=1, keepdims=True)
        for k in range(rows.shape[0])
    ]
    return jnp.concatenate(cols, axis=0)


class Dims:
    def __init__(self, n, queries, cache, cand_ids):
        self.n = n
        self.chips = n**3
        self.devices = 2 * self.chips
        self.qd, self.width = queries
        self.held = cache[0]
        self.blocks = self.held // BLOCK
        self.cands = cand_ids[1]
        self.rows = self.devices * self.qd
        self.half = self.rows // 2
        self.groups = self.devices // 8
        self.grows = 8 * self.qd
        self.stat_rows = self.rows // 128
        self.layer = n * n
        self.tile = min(1024, self.held)
        self.cut = self.width // CUTS


def kernel(
    d,
    q_ref,
    cand_ref,
    map_ref,
    rank_ref,
    cache_hbm,
    grad_ref,
    loss_ref,
    c_ref,
    qown,
    qrecv,
    qall,
    table,
    ra,
    ra2,
    rb,
    meta,
    nbuf,
    tbuf,
    sbuf,
    et,
    mbuf,
    zbuf,
    dbuf,
    stat,
    sa,
    stat2,
    sb,
    uv,
    csend,
    crecv,
    psend,
    precv,
    cache_sem,
    qs,
    qr,
    xs,
    xr,
    tas,
    tar,
    tbs,
    tbr,
    sas,
    sar,
    sbs,
    sbr,
    cs,
    cr,
    ps,
    pr,
):
    n = d.n
    z = lax.axis_index("grp")
    shard = lax.axis_index("shard")
    x = lax.div(shard, 2 * n)
    y = lax.rem(lax.div(shard, 2), n)
    c = lax.rem(shard, 2)
    scale = 3.0 / math.sqrt(d.width)
    xc = x * 2 + c
    yz = y * n + z
    chip = z * d.layer + lax.div(shard, 2)
    nxc, nyz = 2 * n, n * n

    def dev(xx, yy, zz, cc):
        return (zz, (xx * n + yy) * 2 + cc)

    def dev_xc(j):
        return dev(lax.div(j, 2), y, z, lax.rem(j, 2))

    def dev_yz(j):
        return dev(x, lax.div(j, n), lax.rem(j, n), c)

    def other(k):
        h = lax.rem(chip + k, d.chips)
        return (lax.div(h, d.layer), lax.rem(h, d.layer) * 2 + c), h

    sibling = dev(x, y, z, 1 - c)

    barrier = pltpu.get_barrier_semaphore()

    def greet(k, _):
        to, _ = other(k)
        pl.semaphore_signal(barrier, inc=1, device_id=to, device_id_type=MESH)
        return 0

    lax.fori_loop(1, d.chips, greet, 0)
    other_core = 0
    for k in range(1, nxc):
        if k % 2:
            other_core += 1
            pl.semaphore_signal(barrier, inc=1, device_id=dev_xc(lax.rem(xc + k, nxc)), device_id_type=MESH)

    cache_copy = pltpu.make_async_copy(cache_hbm, c_ref, cache_sem)
    cache_copy.start()

    pending = []

    def remote(src, dst, ssem, rsem, to):
        return pltpu.make_async_remote_copy(
            src_ref=src, dst_ref=dst, send_sem=ssem, recv_sem=rsem, device_id=to, device_id_type=MESH
        )

    def send(src, dst, ssem, rsem, to):
        copy = remote(src, dst, ssem, rsem, to)
        copy.start()
        pending.append(copy)

    def arrived(dst, rsem):
        remote(dst, dst, rsem, rsem, sibling).wait_recv()

    def sent(src, ssem):
        remote(src, src, ssem, ssem, sibling).wait_send()

    q16 = q_ref[...].astype(BF16)
    qown[...] = q16
    qrecv[chip] = q16

    teach = -rank_ref[...].astype(F32) * (8.0 / d.cands)
    teach = teach - jnp.max(teach, axis=1, keepdims=True)
    teacher_log = teach - jnp.log(jnp.sum(jnp.exp(teach), axis=1, keepdims=True))
    prob = jnp.exp(teacher_log)
    entropy = jnp.sum(prob * teacher_log, axis=1, keepdims=True)
    prob_hi = prob.astype(BF16).astype(F32)
    prob_lo = prob - prob_hi

    cand = cand_ref[...]
    blk, off = cand // BLOCK, cand % BLOCK
    omap = map_ref[...]
    map_rows = omap.shape[0]
    halves = jnp.concatenate([omap // 64, omap % 64], axis=0).astype(F32).astype(BF16)
    upper = hot(iota((d.cands, d.cands), 0) < iota((d.cands, d.cands), 1))
    total = jnp.zeros((d.devices, 1), F32)
    acc = jnp.zeros((d.devices, 128), F32)
    for i in range(d.qd):
        bi = blk[i : i + 1]
        low = hot(iota((128, d.cands), 0) == bi % 128)
        got = nn(halves, low)
        high = jnp.where(iota((map_rows, d.cands), 0) == bi // 128, 1.0, 0.0)
        pblk = (
            jnp.sum(got[:map_rows] * high, axis=0, keepdims=True) * 64.0
            + jnp.sum(got[map_rows:] * high, axis=0, keepdims=True)
        ).astype(I32)
        owner, lblk = pblk // d.blocks, pblk % d.blocks
        oz, oshard = owner // (2 * n * n), owner % (2 * n * n)
        place = ((oshard // (2 * n)) * 2 + oshard % 2) * nyz + ((oshard // 2) % n) * n + oz
        mine = jnp.where(iota((d.devices, d.cands), 0) == place, 1.0, 0.0)
        mine16 = mine.astype(BF16)
        earlier = nn(mine16, upper) + total
        pos = jnp.sum(mine * earlier, axis=0, keepdims=True).astype(I32)
        total = total + jnp.sum(mine, axis=1, keepdims=True)
        at = jnp.where(iota((CAP, d.cands), 0) == pos, 1.0, 0.0)
        planes = jnp.concatenate(
            [
                at * lblk.astype(F32),
                at * off[i : i + 1].astype(F32),
                at * float(i),
                at * prob_hi[i : i + 1],
                at * prob_lo[i : i + 1],
                jnp.zeros((128 - 5 * CAP, d.cands), F32),
            ],
            axis=0,
        ).astype(BF16)
        acc = acc + nt(mine16, planes)
    table[...] = acc

    pl.semaphore_wait(barrier, d.chips - 1 + other_core)

    for k in range(1, nxc):
        j = lax.rem(xc + k, nxc)
        send(
            table.at[pl.ds(pl.multiple_of(j * nyz, nyz), nyz)],
            ra.at[pl.ds(pl.multiple_of(xc * nyz, nyz), nyz)],
            tas.at[k],
            tar.at[k],
            dev_xc(j),
        )

    def give(k, _):
        to, _ = other(k)
        remote(qown, qrecv.at[chip], qs.at[0], qr.at[z], to).start()
        return 0

    lax.fori_loop(1, d.chips, give, 0)
    own = pl.ds(pl.multiple_of(xc * nyz, nyz), nyz)
    ra[own] = table[own]
    for k in range(1, nxc):
        src = lax.rem(xc + nxc - k, nxc)
        arrived(ra.at[pl.ds(pl.multiple_of(src * nyz, nyz), nyz)], tar.at[k])

    r, s = iota((d.devices, d.devices), 0), iota((d.devices, d.devices), 1)
    perm = hot((r % nxc) * nyz + r // nxc == s)
    ra2[...] = nn(perm, ra[...].astype(BF16))
    for k in range(1, nyz):
        j = lax.rem(yz + k, nyz)
        send(
            ra2.at[pl.ds(pl.multiple_of(j * nxc, nxc), nxc)],
            rb.at[pl.ds(pl.multiple_of(yz * nxc, nxc), nxc)],
            tbs.at[k],
            tbr.at[k],
            dev_yz(j),
        )
    own = pl.ds(pl.multiple_of(yz * nxc, nxc), nxc)
    rb[own] = ra2[own]

    per = max(1, 16 // d.qd)
    for k in range(n):
        layer = lax.rem(z + k, n)
        count = d.layer - 1 if k == 0 else d.layer
        arrived(qrecv.at[pl.ds(layer * d.layer, count)], qr.at[layer])

        def place(i, _, layer=layer):
            first = layer * d.layer + i * per
            rows = [qrecv[first + j].astype(F32) for j in range(per)]
            at = pl.multiple_of(first * d.qd, per * d.qd)
            qall[pl.ds(at, per * d.qd)] = jnp.concatenate(rows, axis=0).astype(BF16)
            return 0

        lax.fori_loop(0, d.layer // per, place, 0)
        size = d.layer * d.qd
        here = pl.ds(pl.multiple_of(layer * size, size), size)
        there = pl.ds(pl.multiple_of(d.half + layer * size, size), size)
        send(qall.at[here], qall.at[there], xs.at[k], xr.at[layer], sibling)

    for k in range(1, nyz):
        src = lax.rem(yz + nyz - k, nyz)
        arrived(rb.at[pl.ds(pl.multiple_of(src * nxc, nxc), nxc)], tbr.at[k])

    rc = jnp.where(r < d.chips, c, 1 - c)
    rh = r % d.chips
    rz, rx, ry = rh // d.layer, (rh // n) % n, rh % n
    perm = hot(((ry * n + rz) * n + rx) * 2 + rc == s)
    lists = nn(perm, rb[...].astype(BF16)).astype(BF16)
    lane = iota((128, 128), 1)
    sub = iota((128, 128), 0)
    pick = jnp.where(iota((d.devices, 128), 0) % 8 == iota((d.devices, 128), 1) // CAP, 1.0, 0.0)
    for p in range(5):
        spread = nn(lists, hot(sub == p * CAP + lane % CAP)) * pick
        meta[p] = jnp.sum(spread.reshape(d.groups, 8, 128), axis=1)

    def fill(g, _):
        lb, lo, lq, hi, low = [meta[p, pl.ds(g, 1), :] for p in range(5)]
        key = lb.astype(I32) * d.grows + (iota((1, 128), 1) // CAP) * d.qd + lq.astype(I32)
        same = iota((128, 128), 0) == lo.astype(I32)
        zero = jnp.zeros((128, 128), F32)
        right = jnp.concatenate(
            [
                jnp.concatenate([jnp.where(same & (hi > 0.0), 1.0, 0.0), zero], axis=1),
                jnp.concatenate([jnp.where(same, hi, 0.0), jnp.where(same, low, 0.0)], axis=1),
            ],
            axis=0,
        ).astype(BF16)
        step = max(1, 256 // d.grows)
        for c0 in range(0, d.blocks, step):
            left = hot(iota((step * d.grows, 128), 0) + c0 * d.grows == key)
            out = nt(jnp.concatenate([left, left], axis=1), right)
            rows = pl.ds(pl.multiple_of(g * d.grows, d.grows), d.grows)
            for k in range(step):
                cols = slice((c0 + k) * 128, (c0 + k + 1) * 128)
                nbuf[rows, cols] = out[k * d.grows : (k + 1) * d.grows, :128]
                tp = out[k * d.grows : (k + 1) * d.grows, 128:]
                tbuf[rows, cols] = tp
                et[pl.ds(pl.multiple_of(d.rows + g * d.grows, d.grows), d.grows), cols] = tp.astype(BF16)
        return 0

    lax.fori_loop(0, d.groups, fill, 0, unroll=min(4, d.groups))

    cache_copy.wait()
    cache_waited = True

    mbuf[...] = jnp.full(mbuf.shape, NEG, F32)
    zbuf[...] = jnp.zeros(zbuf.shape, F32)
    dbuf[...] = jnp.zeros(dbuf.shape, F32)
    halves = [slice(0, d.half), slice(d.half, d.rows)]
    tiles = [slice(t, t + d.tile) for t in range(0, d.held, d.tile)]
    step = min(64, d.half)

    def score(rows, cols):
        sbuf[rows, cols] = nt(qall[rows], c_ref[cols])

    def lanes(cols):
        return [slice(k, k + 128) for k in range(cols.start, cols.stop, 128)]

    def blocks(rows):
        return [slice(r, r + step) for r in range(rows.start, rows.stop, step)]

    def largest(rows, cols):
        for rr in blocks(rows):
            best, dot = mbuf[rr], dbuf[rr]
            for cc in lanes(cols):
                logits = sbuf[rr, cc] * scale
                dot = dot + tbuf[rr, cc] * logits
                best = jnp.maximum(best, jnp.where(nbuf[rr, cc] > 0.0, logits, NEG))
            mbuf[rr] = best
            dbuf[rr] = dot

    def widest(rows):
        mbuf[rows] = jnp.broadcast_to(jnp.max(mbuf[rows], axis=1, keepdims=True), (d.half, 128))

    def expo(rows, cols):
        for rr in blocks(rows):
            top, total = mbuf[rr], zbuf[rr]
            for cc in lanes(cols):
                e = nbuf[rr, cc] * jnp.exp(jnp.minimum(sbuf[rr, cc] * scale - top, 0.0))
                et[rr, cc] = e.astype(BF16)
                total = total + e
            zbuf[rr] = total

    for h in range(2):
        if h == 1:
            for layer in range(n):
                size = d.layer * d.qd
                arrived(qall.at[pl.ds(d.half + layer * size, size)], xr.at[layer])
        for cols in tiles:
            score(halves[h], cols)
        for cols in tiles:
            largest(halves[h], cols)
        widest(halves[h])
        for cols in tiles:
            expo(halves[h], cols)

    nr = d.stat_rows
    my_top = col_to_rows(mbuf[:, :1])
    packed = [
        my_top,
        col_to_rows(jnp.sum(zbuf[...], axis=1, keepdims=True)),
        col_to_rows(jnp.sum(dbuf[...], axis=1, keepdims=True)),
    ]
    spare = [jnp.zeros((16 - 3 * nr, 128), F32)] if 16 - 3 * nr else []
    stat[...] = jnp.concatenate(packed + spare, axis=0)

    def swap(v):
        return jnp.concatenate([v[nr // 2 :], v[: nr // 2]], axis=0)

    def combine(pieces):
        tops = [p[0] for p in pieces]
        best = functools.reduce(jnp.maximum, tops)
        zs = sum(p[1] * jnp.exp(t - best) for p, t in zip(pieces, tops))
        ds = sum(p[2] for p in pieces)
        return best, zs, ds

    def three(v):
        return [v[:nr], v[nr : 2 * nr], v[2 * nr : 3 * nr]]

    for k in range(1, nxc):
        send(stat, sa.at[k], sas.at[k], sar.at[k], dev_xc(lax.rem(xc + k, nxc)))

    def product(t, _):
        cols = pl.ds(pl.multiple_of(t * 256, 256), 256)
        uv[:, cols] = nn(et[...], c_ref[:, cols])
        return 0

    steps = d.width // 256
    lax.fori_loop(0, steps // 2, product, 0)
    for k in range(1, nxc):
        arrived(sa.at[k], sar.at[k])
    pieces = [three(stat[...])]
    for k in range(1, nxc):
        got = three(sa[k])
        pieces.append([swap(v) for v in got] if k % 2 else got)
    stat2[...] = jnp.concatenate(list(combine(pieces)) + spare, axis=0)
    for k in range(1, nyz):
        send(stat2, sb.at[k], sbs.at[k], sbr.at[k], dev_yz(lax.rem(yz + k, nyz)))
    lax.fori_loop(steps // 2, steps, product, 0)
    for k in range(1, nyz):
        arrived(sb.at[k], sbr.at[k])
    best, zs, ds = combine([three(stat2[...])] + [three(sb[k]) for k in range(1, nyz)])

    zbuf[...] = jnp.broadcast_to(rows_to_col(scale * jnp.exp(my_top - best) / zs), zbuf.shape)

    def part(rows, cols):
        wide = jnp.concatenate([zbuf[rows]] * (d.cut // 128), axis=1)
        return uv[rows, cols] * wide - uv[slice(d.rows + rows.start, d.rows + rows.stop), cols] * scale

    cuts = [slice(i * d.cut, (i + 1) * d.cut) for i in range(CUTS)]
    for i in range(CUTS):
        csend[i] = part(halves[1], cuts[i]).astype(BF16)
        send(csend.at[i], crecv.at[i], cs.at[i], cr.at[i], sibling)

    for i in range(CUTS):
        mine = part(halves[0], cuts[i])
        arrived(crecv.at[i], cr.at[i])
        uv[halves[0], cuts[i]] = mine + crecv[i].astype(F32)
        size = max(8, d.qd)

        def split(j, _, i=i):
            rows = uv[pl.ds(pl.multiple_of(j * size, size), size), cuts[i]]
            for k in range(size // d.qd):
                psend[i, j * (size // d.qd) + k] = rows[k * d.qd : (k + 1) * d.qd].astype(BF16)
            return 0

        lax.fori_loop(0, d.half // size, split, 0, unroll=4)
        precv[i, chip] = psend[i, chip]

        def give_back(k, _, i=i):
            to, h = other(k)
            remote(psend.at[i, h], precv.at[i, chip], ps.at[i], pr.at[i], to).start()
            return 0

        lax.fori_loop(1, d.chips, give_back, 0)

    losses = best + jnp.log(zs) - ds
    flat = iota((nr, 128), 0) * 128 + iota((nr, 128), 1)
    out = jnp.zeros((1, 128), F32)
    for i in range(d.qd):
        value = jnp.sum(
            jnp.sum(jnp.where(flat == chip * d.qd + i, losses, 0.0), axis=0, keepdims=True),
            axis=1,
            keepdims=True,
        )
        out = jnp.where(iota((1, 128), 1) == i, value + entropy[i : i + 1], out)
    loss_ref[...] = out[:, : d.qd]

    for i in range(CUTS):
        arrived(precv.at[i, pl.ds(0, d.chips - 1)], pr.at[i])
        grad_ref[:, cuts[i]] = lax.fori_loop(
            0,
            d.chips,
            lambda h, total, i=i: total + precv[i, h].astype(F32),
            jnp.zeros((d.qd, d.cut), F32),
            unroll=8,
        )

    for copy in pending:
        copy.wait_send()
    sent(qrecv.at[pl.ds(0, d.chips - 1)], qs.at[0])
    for i in range(CUTS):
        sent(psend.at[i, pl.ds(0, d.chips - 1)], ps.at[i])


def hand_over(grad_ref, loss_ref, grad_out, loss_out):
    grad_out[...] = grad_ref[...]
    loss_out[...] = loss_ref[...]


def per_device(n, queries, cache, cand_ids, owner_map, teacher_rank):
    d = Dims(n, queries.shape, cache.shape, cand_ids.shape)
    w = d.width
    nxc, nyz = 2 * n, n * n
    dma = lambda k: [pltpu.SemaphoreType.DMA((k,))] * 2
    vmem = pl.BlockSpec(memory_space=pltpu.VMEM)
    grad, loss = pl.pallas_call(
        functools.partial(kernel, d),
        out_shape=(
            jax.ShapeDtypeStruct((d.qd, w), F32),
            jax.ShapeDtypeStruct((1, d.qd), F32),
        ),
        in_specs=[vmem] * 4 + [pl.BlockSpec(memory_space=pl.ANY)],
        out_specs=(vmem, vmem),
        scratch_shapes=[
            pltpu.VMEM((d.held, w), BF16),
            pltpu.VMEM((d.qd, w), BF16),
            pltpu.VMEM((d.chips, d.qd, w), BF16),
            pltpu.VMEM((d.rows, w), BF16),
            pltpu.VMEM((d.devices, 128), F32),
            pltpu.VMEM((d.devices, 128), F32),
            pltpu.VMEM((d.devices, 128), F32),
            pltpu.VMEM((d.devices, 128), F32),
            pltpu.VMEM((5, d.groups, 128), F32),
            pltpu.VMEM((d.rows, d.held), F32),
            pltpu.VMEM((d.rows, d.held), F32),
            pltpu.VMEM((d.rows, d.held), F32),
            pltpu.VMEM((2 * d.rows, d.held), BF16),
            pltpu.VMEM((d.rows, 128), F32),
            pltpu.VMEM((d.rows, 128), F32),
            pltpu.VMEM((d.rows, 128), F32),
            pltpu.VMEM((16, 128), F32),
            pltpu.VMEM((nxc, 16, 128), F32),
            pltpu.VMEM((16, 128), F32),
            pltpu.VMEM((nyz, 16, 128), F32),
            pltpu.VMEM((2 * d.rows, w), F32),
            pltpu.VMEM((CUTS, d.half, d.cut), BF16),
            pltpu.VMEM((CUTS, d.half, d.cut), BF16),
            pltpu.VMEM((CUTS, d.chips, d.qd, d.cut), BF16),
            pltpu.VMEM((CUTS, d.chips, d.qd, d.cut), BF16),
            pltpu.SemaphoreType.DMA,
            pltpu.SemaphoreType.DMA((1,)),
            pltpu.SemaphoreType.DMA((n,)),
            *dma(n),
            *dma(nxc),
            *dma(nyz),
            *dma(nxc),
            *dma(nyz),
            *dma(CUTS),
            *dma(CUTS),
        ],
        compiler_params=pltpu.CompilerParams(
            collective_id=0, has_side_effects=True, vmem_limit_bytes=60 * 2**20
        ),
    )(queries, cand_ids, owner_map.reshape(-1, 128), teacher_rank, cache)
    grad, loss = pl.pallas_call(
        hand_over,
        out_shape=(
            jax.ShapeDtypeStruct((d.qd, w), F32),
            jax.ShapeDtypeStruct((1, d.qd), F32),
        ),
        in_specs=[vmem] * 2,
        out_specs=(vmem, vmem),
    )(grad, loss)
    return grad, loss.reshape(d.qd)


def solution(mesh):
    n = mesh.shape["grp"]
    both = P(("grp", "shard"), None)
    return jax.shard_map(
        functools.partial(per_device, n),
        mesh=mesh,
        in_specs=(both, both, both, P(), both),
        out_specs=(both, P(("grp", "shard"))),
        check_vma=False,
    )
```

```python
import functools
import math

import jax
import jax.numpy as jnp
from jax import lax
from jax.experimental import pallas as pl
from jax.experimental.pallas import tpu as pltpu
from jax.sharding import PartitionSpec as P

MESH = pl.DeviceIdType.MESH
BLOCK = 128
CAP = 16
CUTS = 2
NEG = -1e30
F32 = jnp.float32
BF16 = jnp.bfloat16
I32 = jnp.int32


def iota(shape, dim):
    return lax.broadcasted_iota(I32, shape, dim)


def nt(a, b):
    return lax.dot_general(a, b, (((1,), (1,)), ((), ())), preferred_element_type=F32)


def nn(a, b):
    return jnp.dot(a, b, preferred_element_type=F32)


def hot(mask):
    return jnp.where(mask, 1.0, 0.0).astype(BF16)


def col_to_rows(col):
    eye = iota((128, 128), 0) == iota((128, 128), 1)
    rows = [
        jnp.sum(jnp.where(eye, col[k * 128 : (k + 1) * 128], 0.0), axis=0, keepdims=True)
        for k in range(col.shape[0] // 128)
    ]
    return jnp.concatenate(rows, axis=0)


def rows_to_col(rows):
    eye = iota((128, 128), 0) == iota((128, 128), 1)
    cols = [
        jnp.sum(jnp.where(eye, rows[k : k + 1], 0.0), axis=1, keepdims=True)
        for k in range(rows.shape[0])
    ]
    return jnp.concatenate(cols, axis=0)


class Dims:
    def __init__(self, n, queries, cache, cand_ids):
        self.n = n
        self.chips = n**3
        self.devices = 2 * self.chips
        self.qd, self.width = queries
        self.held = cache[0]
        self.blocks = self.held // BLOCK
        self.cands = cand_ids[1]
        self.rows = self.devices * self.qd
        self.half = self.rows // 2
        self.groups = self.devices // 8
        self.grows = 8 * self.qd
        self.stat_rows = self.rows // 128
        self.layer = n * n
        self.tile = min(1024, self.held)
        self.cut = self.width // CUTS


def kernel(
    d,
    q_hbm,
    cand_hbm,
    map_hbm,
    rank_hbm,
    cache_hbm,
    grad_ref,
    loss_ref,
    q_ref,
    cand_ref,
    map_ref,
    rank_ref,
    c_ref,
    qown,
    qrecv,
    qall,
    table,
    ra,
    ra2,
    rb,
    meta,
    nbuf,
    tbuf,
    sbuf,
    et,
    mbuf,
    zbuf,
    dbuf,
    stat,
    sa,
    stat2,
    sb,
    uv,
    csend,
    crecv,
    psend,
    precv,
    small_sem,
    cache_sem,
    qs,
    qr,
    xs,
    xr,
    tas,
    tar,
    tbs,
    tbr,
    sas,
    sar,
    sbs,
    sbr,
    cs,
    cr,
    ps,
    pr,
):
    n = d.n
    z = lax.axis_index("grp")
    shard = lax.axis_index("shard")
    x = lax.div(shard, 2 * n)
    y = lax.rem(lax.div(shard, 2), n)
    c = lax.rem(shard, 2)
    scale = 3.0 / math.sqrt(d.width)
    xc = x * 2 + c
    yz = y * n + z
    chip = z * d.layer + lax.div(shard, 2)
    nxc, nyz = 2 * n, n * n

    def dev(xx, yy, zz, cc):
        return (zz, (xx * n + yy) * 2 + cc)

    def dev_xc(j):
        return dev(lax.div(j, 2), y, z, lax.rem(j, 2))

    def dev_yz(j):
        return dev(x, lax.div(j, n), lax.rem(j, n), c)

    away = sorted(range(n), key=lambda v: -min(v, n - v))

    def ahead(at, t):
        by = away[-1]
        for i in range(n - 1):
            by = jnp.where(t == i, away[i], by)
        return lax.rem(at + by, n)

    def other(k):
        zz = ahead(z, lax.div(k, d.layer))
        xx = ahead(x, lax.rem(lax.div(k, n), n))
        yy = ahead(y, lax.rem(k, n))
        h = xx * n + yy
        return (zz, h * 2 + c), zz * d.layer + h

    far_xc = sorted(range(1, nxc), key=lambda k: -min(k, nxc - k))
    far_yz = sorted(range(1, nyz), key=lambda k: -min(k // n, n - k // n) - min(k % n, n - k % n))

    sibling = dev(x, y, z, 1 - c)

    small = [
        pltpu.make_async_copy(src, dst, small_sem.at[i])
        for i, (src, dst) in enumerate(
            [(cand_hbm, cand_ref), (map_hbm, map_ref), (rank_hbm, rank_ref), (q_hbm, q_ref)]
        )
    ]
    for copy in small:
        copy.start()

    barrier = pltpu.get_barrier_semaphore()

    def greet(k, _):
        to, _ = other(k)
        pl.semaphore_signal(barrier, inc=1, device_id=to, device_id_type=MESH)
        return 0

    lax.fori_loop(0, d.chips - 1, greet, 0)
    other_core = 0
    for k in range(1, nxc):
        if k % 2:
            other_core += 1
            pl.semaphore_signal(barrier, inc=1, device_id=dev_xc(lax.rem(xc + k, nxc)), device_id_type=MESH)

    cache_copy = pltpu.make_async_copy(cache_hbm, c_ref, cache_sem)
    cache_copy.start()

    pending = []

    def remote(src, dst, ssem, rsem, to):
        return pltpu.make_async_remote_copy(
            src_ref=src, dst_ref=dst, send_sem=ssem, recv_sem=rsem, device_id=to, device_id_type=MESH
        )

    def send(src, dst, ssem, rsem, to):
        copy = remote(src, dst, ssem, rsem, to)
        copy.start()
        pending.append(copy)

    def arrived(dst, rsem):
        remote(dst, dst, rsem, rsem, sibling).wait_recv()

    def sent(src, ssem):
        remote(src, src, ssem, ssem, sibling).wait_send()

    for copy in small:
        copy.wait()
    q16 = q_ref[...].astype(BF16)
    qown[...] = q16
    qrecv[chip] = q16

    teach = -rank_ref[...].astype(F32) * (8.0 / d.cands)
    teach = teach - jnp.max(teach, axis=1, keepdims=True)
    teacher_log = teach - jnp.log(jnp.sum(jnp.exp(teach), axis=1, keepdims=True))
    prob = jnp.exp(teacher_log)
    entropy = jnp.sum(prob * teacher_log, axis=1, keepdims=True)
    prob_hi = prob.astype(BF16).astype(F32)
    prob_lo = prob - prob_hi

    cand = cand_ref[...]
    blk, off = cand // BLOCK, cand % BLOCK
    omap = map_ref[...]
    map_rows = omap.shape[0]
    halves = jnp.concatenate([omap // 64, omap % 64], axis=0).astype(F32).astype(BF16)
    upper = hot(iota((d.cands, d.cands), 0) < iota((d.cands, d.cands), 1))
    total = jnp.zeros((d.devices, 1), F32)
    acc = jnp.zeros((d.devices, 128), F32)
    for i in range(d.qd):
        bi = blk[i : i + 1]
        low = hot(iota((128, d.cands), 0) == bi % 128)
        got = nn(halves, low)
        high = jnp.where(iota((map_rows, d.cands), 0) == bi // 128, 1.0, 0.0)
        pblk = (
            jnp.sum(got[:map_rows] * high, axis=0, keepdims=True) * 64.0
            + jnp.sum(got[map_rows:] * high, axis=0, keepdims=True)
        ).astype(I32)
        owner, lblk = pblk // d.blocks, pblk % d.blocks
        place = (owner % 2) * d.chips + owner // 2
        mine = jnp.where(iota((d.devices, d.cands), 0) == place, 1.0, 0.0)
        mine16 = mine.astype(BF16)
        earlier = nn(mine16, upper) + total
        pos = jnp.sum(mine * earlier, axis=0, keepdims=True).astype(I32)
        total = total + jnp.sum(mine, axis=1, keepdims=True)
        at = jnp.where(iota((CAP, d.cands), 0) == pos, 1.0, 0.0)
        planes = jnp.concatenate(
            [
                at * lblk.astype(F32),
                at * off[i : i + 1].astype(F32),
                at * float(i),
                at * prob_hi[i : i + 1],
                at * prob_lo[i : i + 1],
                jnp.zeros((128 - 5 * CAP, d.cands), F32),
            ],
            axis=0,
        ).astype(BF16)
        acc = acc + nt(mine16, planes)
    for core in range(2):
        table[:, core, :] = acc[core * d.chips : (core + 1) * d.chips]
    ra[chip] = table[chip]

    pl.semaphore_wait(barrier, d.chips - 1 + other_core)

    def ask(k, _):
        to, h = other(k)
        remote(table.at[h], ra.at[chip], tas.at[0], tar.at[0], to).start()
        return 0

    lax.fori_loop(0, d.chips - 1, ask, 0)

    def give(k, _):
        to, _ = other(k)
        remote(qown, qrecv.at[chip], qs.at[0], qr.at[z], to).start()
        return 0

    lax.fori_loop(0, d.chips - 1, give, 0)
    arrived(ra.at[pl.ds(0, d.chips - 1)], tar.at[0])
    pair = [ra[:, core, :] for core in range(2)]
    ra2[...] = jnp.where(c == 0, pair[1], pair[0])
    send(ra2, rb.at[pl.ds(d.chips, d.chips)], tbs.at[0], tbr.at[0], sibling)
    rb[: d.chips] = jnp.where(c == 0, pair[0], pair[1])
    arrived(rb.at[pl.ds(d.chips, d.chips)], tbr.at[0])
    lists = rb[...].astype(BF16)
    lane = iota((128, 128), 1)
    sub = iota((128, 128), 0)
    pick = jnp.where(iota((d.devices, 128), 0) % 8 == iota((d.devices, 128), 1) // CAP, 1.0, 0.0)
    for p in range(5):
        spread = nn(lists, hot(sub == p * CAP + lane % CAP)) * pick
        meta[p] = jnp.sum(spread.reshape(d.groups, 8, 128), axis=1)

    def fill(g, _):
        lb, lo, lq, hi, low = [meta[p, pl.ds(g, 1), :] for p in range(5)]
        key = lb.astype(I32) * d.grows + (iota((1, 128), 1) // CAP) * d.qd + lq.astype(I32)
        same = iota((128, 128), 0) == lo.astype(I32)
        zero = jnp.zeros((128, 128), F32)
        right = jnp.concatenate(
            [
                jnp.concatenate([jnp.where(same & (hi > 0.0), 1.0, 0.0), zero], axis=1),
                jnp.concatenate([jnp.where(same, hi, 0.0), jnp.where(same, low, 0.0)], axis=1),
            ],
            axis=0,
        ).astype(BF16)
        step = max(1, 256 // d.grows)
        for c0 in range(0, d.blocks, step):
            left = hot(iota((step * d.grows, 128), 0) + c0 * d.grows == key)
            out = nt(jnp.concatenate([left, left], axis=1), right)
            rows = pl.ds(pl.multiple_of(g * d.grows, d.grows), d.grows)
            for k in range(step):
                cols = slice((c0 + k) * 128, (c0 + k + 1) * 128)
                nbuf[rows, cols] = out[k * d.grows : (k + 1) * d.grows, :128]
                tp = out[k * d.grows : (k + 1) * d.grows, 128:]
                tbuf[rows, cols] = tp
                et[pl.ds(pl.multiple_of(d.rows + g * d.grows, d.grows), d.grows), cols] = tp.astype(BF16)
        return 0

    lax.fori_loop(0, d.groups, fill, 0, unroll=min(8, d.groups))

    per = max(1, 16 // d.qd)
    for k in range(n):
        layer = lax.rem(z + k, n)
        count = d.layer - 1 if k == 0 else d.layer
        arrived(qrecv.at[pl.ds(layer * d.layer, count)], qr.at[layer])

        def place(i, _, layer=layer):
            first = layer * d.layer + i * per
            rows = [qrecv[first + j].astype(F32) for j in range(per)]
            at = pl.multiple_of(first * d.qd, per * d.qd)
            qall[pl.ds(at, per * d.qd)] = jnp.concatenate(rows, axis=0).astype(BF16)
            return 0

        lax.fori_loop(0, d.layer // per, place, 0, unroll=True)
        size = d.layer * d.qd
        here = pl.ds(pl.multiple_of(layer * size, size), size)
        there = pl.ds(pl.multiple_of(d.half + layer * size, size), size)
        send(qall.at[here], qall.at[there], xs.at[k], xr.at[layer], sibling)

    cache_copy.wait()
    cache_waited = True

    mbuf[...] = jnp.full(mbuf.shape, NEG, F32)
    zbuf[...] = jnp.zeros(zbuf.shape, F32)
    dbuf[...] = jnp.zeros(dbuf.shape, F32)
    halves = [slice(0, d.half), slice(d.half, d.rows)]
    tiles = [slice(t, t + d.tile) for t in range(0, d.held, d.tile)]
    step = min(64, d.half)

    def score(rows, cols):
        sbuf[rows, cols] = nt(qall[rows], c_ref[cols])

    def lanes(cols):
        return [slice(k, k + 128) for k in range(cols.start, cols.stop, 128)]

    def blocks(rows):
        return [slice(r, r + step) for r in range(rows.start, rows.stop, step)]

    def largest(rows, cols):
        for rr in blocks(rows):
            best, dot = mbuf[rr], dbuf[rr]
            for cc in lanes(cols):
                logits = sbuf[rr, cc] * scale
                dot = dot + tbuf[rr, cc] * logits
                best = jnp.maximum(best, jnp.where(nbuf[rr, cc] > 0.0, logits, NEG))
            mbuf[rr] = best
            dbuf[rr] = dot

    def widest(rows):
        mbuf[rows] = jnp.broadcast_to(jnp.max(mbuf[rows], axis=1, keepdims=True), (d.half, 128))

    def expo(rows, cols):
        for rr in blocks(rows):
            top, total = mbuf[rr], zbuf[rr]
            for cc in lanes(cols):
                e = nbuf[rr, cc] * jnp.exp(jnp.minimum(sbuf[rr, cc] * scale - top, 0.0))
                et[rr, cc] = e.astype(BF16)
                total = total + e
            zbuf[rr] = total

    for h in range(2):
        if h == 1:
            for layer in range(n):
                size = d.layer * d.qd
                arrived(qall.at[pl.ds(d.half + layer * size, size)], xr.at[layer])
        for cols in tiles:
            score(halves[h], cols)
        for cols in tiles:
            largest(halves[h], cols)
        widest(halves[h])
        for cols in tiles:
            expo(halves[h], cols)

    nr = d.stat_rows
    my_top = col_to_rows(mbuf[:, :1])
    packed = [
        my_top,
        col_to_rows(jnp.sum(zbuf[...], axis=1, keepdims=True)),
        col_to_rows(jnp.sum(dbuf[...], axis=1, keepdims=True)),
    ]
    spare = [jnp.zeros((16 - 3 * nr, 128), F32)] if 16 - 3 * nr else []
    stat[...] = jnp.concatenate(packed + spare, axis=0)

    def swap(v):
        return jnp.concatenate([v[nr // 2 :], v[: nr // 2]], axis=0)

    def combine(pieces):
        tops = [p[0] for p in pieces]
        best = functools.reduce(jnp.maximum, tops)
        zs = sum(p[1] * jnp.exp(t - best) for p, t in zip(pieces, tops))
        ds = sum(p[2] for p in pieces)
        return best, zs, ds

    def three(v):
        return [v[:nr], v[nr : 2 * nr], v[2 * nr : 3 * nr]]

    for k in far_xc:
        send(stat, sa.at[k], sas.at[k], sar.at[k], dev_xc(lax.rem(xc + k, nxc)))

    def product(t, _):
        cols = pl.ds(pl.multiple_of(t * 256, 256), 256)
        uv[:, cols] = nn(et[...], c_ref[:, cols])
        return 0

    steps = d.width // 256
    lax.fori_loop(0, steps // 2, product, 0)
    for k in range(1, nxc):
        arrived(sa.at[k], sar.at[k])
    pieces = [three(stat[...])]
    for k in range(1, nxc):
        got = three(sa[k])
        pieces.append([swap(v) for v in got] if k % 2 else got)
    stat2[...] = jnp.concatenate(list(combine(pieces)) + spare, axis=0)
    for k in far_yz:
        send(stat2, sb.at[k], sbs.at[k], sbr.at[k], dev_yz(lax.rem(yz + k, nyz)))
    lax.fori_loop(steps // 2, steps, product, 0)
    for k in range(1, nyz):
        arrived(sb.at[k], sbr.at[k])
    best, zs, ds = combine([three(stat2[...])] + [three(sb[k]) for k in range(1, nyz)])

    zbuf[...] = jnp.broadcast_to(rows_to_col(scale * jnp.exp(my_top - best) / zs), zbuf.shape)

    def part(rows, cols):
        wide = jnp.concatenate([zbuf[rows]] * (d.cut // 128), axis=1)
        return uv[rows, cols] * wide - uv[slice(d.rows + rows.start, d.rows + rows.stop), cols] * scale

    cuts = [slice(i * d.cut, (i + 1) * d.cut) for i in range(CUTS)]
    for i in range(CUTS):
        csend[i] = part(halves[1], cuts[i]).astype(BF16)
        send(csend.at[i], crecv.at[i], cs.at[i], cr.at[i], sibling)

    for i in range(CUTS):
        mine = part(halves[0], cuts[i])
        arrived(crecv.at[i], cr.at[i])
        uv[halves[0], cuts[i]] = mine + crecv[i].astype(F32)
        size = max(8, d.qd)

        def split(j, _, i=i):
            rows = uv[pl.ds(pl.multiple_of(j * size, size), size), cuts[i]]
            for k in range(size // d.qd):
                psend[i, j * (size // d.qd) + k] = rows[k * d.qd : (k + 1) * d.qd].astype(BF16)
            return 0

        lax.fori_loop(0, d.half // size, split, 0, unroll=4)
        precv[i, chip] = psend[i, chip]

        def give_back(k, _, i=i):
            to, h = other(k)
            remote(psend.at[i, h], precv.at[i, chip], ps.at[i], pr.at[i], to).start()
            return 0

        lax.fori_loop(0, d.chips - 1, give_back, 0)

    losses = best + jnp.log(zs) - ds
    flat = iota((nr, 128), 0) * 128 + iota((nr, 128), 1)
    out = jnp.zeros((1, 128), F32)
    for i in range(d.qd):
        value = jnp.sum(
            jnp.sum(jnp.where(flat == chip * d.qd + i, losses, 0.0), axis=0, keepdims=True),
            axis=1,
            keepdims=True,
        )
        out = jnp.where(iota((1, 128), 1) == i, value + entropy[i : i + 1], out)
    loss_ref[...] = out[:, : d.qd]

    for i in range(CUTS):
        arrived(precv.at[i, pl.ds(0, d.chips - 1)], pr.at[i])
        grad_ref[:, cuts[i]] = lax.fori_loop(
            0,
            d.chips,
            lambda h, total, i=i: total + precv[i, h].astype(F32),
            jnp.zeros((d.qd, d.cut), F32),
            unroll=8,
        )

    for copy in pending:
        copy.wait_send()
    sent(qrecv.at[pl.ds(0, d.chips - 1)], qs.at[0])
    sent(ra.at[pl.ds(0, d.chips - 1)], tas.at[0])
    for i in range(CUTS):
        sent(psend.at[i, pl.ds(0, d.chips - 1)], ps.at[i])


def hand_over(grad_ref, loss_ref, grad_out, loss_out):
    grad_out[...] = grad_ref[...]
    loss_out[...] = loss_ref[...]


def per_device(n, queries, cache, cand_ids, owner_map, teacher_rank):
    d = Dims(n, queries.shape, cache.shape, cand_ids.shape)
    w = d.width
    nxc, nyz = 2 * n, n * n
    dma = lambda k: [pltpu.SemaphoreType.DMA((k,))] * 2
    vmem = pl.BlockSpec(memory_space=pltpu.VMEM)
    grad, loss = pl.pallas_call(
        functools.partial(kernel, d),
        out_shape=(
            jax.ShapeDtypeStruct((d.qd, w), F32),
            jax.ShapeDtypeStruct((1, d.qd), F32),
        ),
        in_specs=[pl.BlockSpec(memory_space=pl.ANY)] * 5,
        out_specs=(vmem, vmem),
        scratch_shapes=[
            pltpu.VMEM((d.qd, w), F32),
            pltpu.VMEM((d.qd, d.cands), I32),
            pltpu.VMEM((owner_map.shape[0] // 128, 128), I32),
            pltpu.VMEM((d.qd, d.cands), I32),
            pltpu.VMEM((d.held, w), BF16),
            pltpu.VMEM((d.qd, w), BF16),
            pltpu.VMEM((d.chips, d.qd, w), BF16),
            pltpu.VMEM((d.rows, w), BF16),
            pltpu.VMEM((d.chips, 2, 128), F32),
            pltpu.VMEM((d.chips, 2, 128), F32),
            pltpu.VMEM((d.chips, 128), F32),
            pltpu.VMEM((d.devices, 128), F32),
            pltpu.VMEM((5, d.groups, 128), F32),
            pltpu.VMEM((d.rows, d.held), F32),
            pltpu.VMEM((d.rows, d.held), F32),
            pltpu.VMEM((d.rows, d.held), F32),
            pltpu.VMEM((2 * d.rows, d.held), BF16),
            pltpu.VMEM((d.rows, 128), F32),
            pltpu.VMEM((d.rows, 128), F32),
            pltpu.VMEM((d.rows, 128), F32),
            pltpu.VMEM((16, 128), F32),
            pltpu.VMEM((nxc, 16, 128), F32),
            pltpu.VMEM((16, 128), F32),
            pltpu.VMEM((nyz, 16, 128), F32),
            pltpu.VMEM((2 * d.rows, w), F32),
            pltpu.VMEM((CUTS, d.half, d.cut), BF16),
            pltpu.VMEM((CUTS, d.half, d.cut), BF16),
            pltpu.VMEM((CUTS, d.chips, d.qd, d.cut), BF16),
            pltpu.VMEM((CUTS, d.chips, d.qd, d.cut), BF16),
            pltpu.SemaphoreType.DMA((4,)),
            pltpu.SemaphoreType.DMA,
            pltpu.SemaphoreType.DMA((1,)),
            pltpu.SemaphoreType.DMA((n,)),
            *dma(n),
            *dma(1),
            *dma(1),
            *dma(nxc),
            *dma(nyz),
            *dma(CUTS),
            *dma(CUTS),
        ],
        compiler_params=pltpu.CompilerParams(
            collective_id=0, has_side_effects=True, vmem_limit_bytes=60 * 2**20
        ),
    )(queries, cand_ids, owner_map.reshape(-1, 128), teacher_rank, cache)
    grad, loss = pl.pallas_call(
        hand_over,
        out_shape=(
            jax.ShapeDtypeStruct((d.qd, w), F32),
            jax.ShapeDtypeStruct((1, d.qd), F32),
        ),
        in_specs=[vmem] * 2,
        out_specs=(vmem, vmem),
    )(grad, loss)
    return grad, loss.reshape(d.qd)


def solution(mesh):
    n = mesh.shape["grp"]
    both = P(("grp", "shard"), None)
    return jax.shard_map(
        functools.partial(per_device, n),
        mesh=mesh,
        in_specs=(both, both, both, P(), both),
        out_specs=(both, P(("grp", "shard"))),
        check_vma=False,
    )
```

```python
import functools
import math

import jax
import jax.numpy as jnp
from jax import lax
from jax.experimental import pallas as pl
from jax.experimental.pallas import tpu as pltpu
from jax.sharding import PartitionSpec as P

MESH = pl.DeviceIdType.MESH
BLOCK = 128
CAP = 16
CUTS = 2
NEG = -1e30
F32 = jnp.float32
BF16 = jnp.bfloat16
I32 = jnp.int32


def iota(shape, dim):
    return lax.broadcasted_iota(I32, shape, dim)


def nt(a, b):
    return lax.dot_general(a, b, (((1,), (1,)), ((), ())), preferred_element_type=F32)


def nn(a, b):
    return jnp.dot(a, b, preferred_element_type=F32)


def hot(mask):
    return jnp.where(mask, 1.0, 0.0).astype(BF16)


def col_to_rows(col):
    eye = iota((128, 128), 0) == iota((128, 128), 1)
    rows = [
        jnp.sum(jnp.where(eye, col[k * 128 : (k + 1) * 128], 0.0), axis=0, keepdims=True)
        for k in range(col.shape[0] // 128)
    ]
    return jnp.concatenate(rows, axis=0)


def rows_to_col(rows):
    eye = iota((128, 128), 0) == iota((128, 128), 1)
    cols = [
        jnp.sum(jnp.where(eye, rows[k : k + 1], 0.0), axis=1, keepdims=True)
        for k in range(rows.shape[0])
    ]
    return jnp.concatenate(cols, axis=0)


class Dims:
    def __init__(self, n, queries, cache, cand_ids):
        self.n = n
        self.chips = n**3
        self.devices = 2 * self.chips
        self.qd, self.width = queries
        self.held = cache[0]
        self.blocks = self.held // BLOCK
        self.cands = cand_ids[1]
        self.rows = self.devices * self.qd
        self.half = self.rows // 2
        self.groups = self.devices // 8
        self.grows = 8 * self.qd
        self.stat_rows = self.rows // 128
        self.layer = n * n
        self.tile = min(1024, self.held)
        self.cut = self.width // CUTS


def kernel(
    d,
    q_hbm,
    cand_hbm,
    map_hbm,
    rank_hbm,
    cache_hbm,
    grad_ref,
    loss_ref,
    q_ref,
    cand_ref,
    map_ref,
    rank_ref,
    c_ref,
    qown,
    qrecv,
    qall,
    table,
    ra,
    ra2,
    rb,
    meta,
    nbuf,
    tbuf,
    sbuf,
    et,
    mbuf,
    zbuf,
    dbuf,
    stat,
    sa,
    stat2,
    sb,
    uv,
    csend,
    crecv,
    psend,
    precv,
    small_sem,
    cache_sem,
    qs,
    qr,
    xs,
    xr,
    tas,
    tar,
    tbs,
    tbr,
    sas,
    sar,
    sbs,
    sbr,
    cs,
    cr,
    ps,
    pr,
):
    n = d.n
    z = lax.axis_index("grp")
    shard = lax.axis_index("shard")
    x = lax.div(shard, 2 * n)
    y = lax.rem(lax.div(shard, 2), n)
    c = lax.rem(shard, 2)
    scale = 3.0 / math.sqrt(d.width)
    xc = x * 2 + c
    yz = y * n + z
    chip = z * d.layer + lax.div(shard, 2)
    nxc, nyz = 2 * n, n * n

    def dev(xx, yy, zz, cc):
        return (zz, (xx * n + yy) * 2 + cc)

    def dev_xc(j):
        return dev(lax.div(j, 2), y, z, lax.rem(j, 2))

    def dev_yz(j):
        return dev(x, lax.div(j, n), lax.rem(j, n), c)

    away = sorted(range(n), key=lambda v: -min(v, n - v))

    def ahead(at, t):
        by = away[-1]
        for i in range(n - 1):
            by = jnp.where(t == i, away[i], by)
        return lax.rem(at + by, n)

    def other(k):
        zz = ahead(z, lax.div(k, d.layer))
        xx = ahead(x, lax.rem(lax.div(k, n), n))
        yy = ahead(y, lax.rem(k, n))
        h = xx * n + yy
        return (zz, h * 2 + c), zz * d.layer + h

    far_xc = sorted(range(1, nxc), key=lambda k: -min(k, nxc - k))
    far_yz = sorted(range(1, nyz), key=lambda k: -min(k // n, n - k // n) - min(k % n, n - k % n))

    sibling = dev(x, y, z, 1 - c)

    small = [
        pltpu.make_async_copy(src, dst, small_sem.at[i])
        for i, (src, dst) in enumerate(
            [(cand_hbm, cand_ref), (map_hbm, map_ref), (rank_hbm, rank_ref), (q_hbm, q_ref)]
        )
    ]
    for copy in small:
        copy.start()

    barrier = pltpu.get_barrier_semaphore()

    def greet(k, _):
        to, _ = other(k)
        pl.semaphore_signal(barrier, inc=1, device_id=to, device_id_type=MESH)
        return 0

    lax.fori_loop(0, d.chips - 1, greet, 0)
    other_core = 0
    for k in range(1, nxc):
        if k % 2:
            other_core += 1
            pl.semaphore_signal(barrier, inc=1, device_id=dev_xc(lax.rem(xc + k, nxc)), device_id_type=MESH)

    cache_copy = pltpu.make_async_copy(cache_hbm, c_ref, cache_sem)
    cache_copy.start()

    pending = []

    def remote(src, dst, ssem, rsem, to):
        return pltpu.make_async_remote_copy(
            src_ref=src, dst_ref=dst, send_sem=ssem, recv_sem=rsem, device_id=to, device_id_type=MESH
        )

    def send(src, dst, ssem, rsem, to):
        copy = remote(src, dst, ssem, rsem, to)
        copy.start()
        pending.append(copy)

    def arrived(dst, rsem):
        remote(dst, dst, rsem, rsem, sibling).wait_recv()

    def sent(src, ssem):
        remote(src, src, ssem, ssem, sibling).wait_send()

    for copy in small:
        copy.wait()
    q16 = q_ref[...].astype(BF16)
    qown[...] = q16
    qrecv[chip] = q16

    teach = -rank_ref[...].astype(F32) * (8.0 / d.cands)
    teach = teach - jnp.max(teach, axis=1, keepdims=True)
    teacher_log = teach - jnp.log(jnp.sum(jnp.exp(teach), axis=1, keepdims=True))
    prob = jnp.exp(teacher_log)
    entropy = jnp.sum(prob * teacher_log, axis=1, keepdims=True)
    prob_hi = prob.astype(BF16).astype(F32)
    prob_lo = prob - prob_hi

    cand = cand_ref[...]
    blk, off = cand // BLOCK, cand % BLOCK
    omap = map_ref[...]
    map_rows = omap.shape[0]
    halves = jnp.concatenate([omap // 64, omap % 64], axis=0).astype(F32).astype(BF16)
    upper = hot(iota((d.cands, d.cands), 0) < iota((d.cands, d.cands), 1))
    total = jnp.zeros((d.devices, 1), F32)
    acc = jnp.zeros((d.devices, 128), F32)
    for i in range(d.qd):
        bi = blk[i : i + 1]
        low = hot(iota((128, d.cands), 0) == bi % 128)
        got = nn(halves, low)
        high = jnp.where(iota((map_rows, d.cands), 0) == bi // 128, 1.0, 0.0)
        pblk = (
            jnp.sum(got[:map_rows] * high, axis=0, keepdims=True) * 64.0
            + jnp.sum(got[map_rows:] * high, axis=0, keepdims=True)
        ).astype(I32)
        owner, lblk = pblk // d.blocks, pblk % d.blocks
        place = (owner % 2) * d.chips + owner // 2
        mine = jnp.where(iota((d.devices, d.cands), 0) == place, 1.0, 0.0)
        mine16 = mine.astype(BF16)
        earlier = nn(mine16, upper) + total
        pos = jnp.sum(mine * earlier, axis=0, keepdims=True).astype(I32)
        total = total + jnp.sum(mine, axis=1, keepdims=True)
        at = jnp.where(iota((CAP, d.cands), 0) == pos, 1.0, 0.0)
        planes = jnp.concatenate(
            [
                at * lblk.astype(F32),
                at * off[i : i + 1].astype(F32),
                at * float(i),
                at * prob_hi[i : i + 1],
                at * prob_lo[i : i + 1],
                jnp.zeros((128 - 5 * CAP, d.cands), F32),
            ],
            axis=0,
        ).astype(BF16)
        acc = acc + nt(mine16, planes)
    for core in range(2):
        table[:, core, :] = acc[core * d.chips : (core + 1) * d.chips]
    ra[chip] = table[chip]

    pl.semaphore_wait(barrier, d.chips - 1 + other_core)

    def ask(k, _):
        to, h = other(k)
        remote(table.at[h], ra.at[chip], tas.at[0], tar.at[0], to).start()
        return 0

    lax.fori_loop(0, d.chips - 1, ask, 0)

    def give(k, _):
        to, _ = other(k)
        remote(qown, qrecv.at[chip], qs.at[0], qr.at[z], to).start()
        return 0

    lax.fori_loop(0, d.chips - 1, give, 0, unroll=3)
    arrived(ra.at[pl.ds(0, d.chips - 1)], tar.at[0])
    pair = [ra[:, core, :] for core in range(2)]
    ra2[...] = jnp.where(c == 0, pair[1], pair[0])
    send(ra2, rb.at[pl.ds(d.chips, d.chips)], tbs.at[0], tbr.at[0], sibling)
    rb[: d.chips] = jnp.where(c == 0, pair[0], pair[1])
    arrived(rb.at[pl.ds(d.chips, d.chips)], tbr.at[0])
    lists = rb[...].astype(BF16)
    lane = iota((128, 128), 1)
    sub = iota((128, 128), 0)
    pick = jnp.where(iota((d.devices, 128), 0) % 8 == iota((d.devices, 128), 1) // CAP, 1.0, 0.0)
    for p in range(5):
        spread = nn(lists, hot(sub == p * CAP + lane % CAP)) * pick
        meta[p] = jnp.sum(spread.reshape(d.groups, 8, 128), axis=1)

    def fill(g, _):
        lb, lo, lq, hi, low = [meta[p, pl.ds(g, 1), :] for p in range(5)]
        key = lb.astype(I32) * d.grows + (iota((1, 128), 1) // CAP) * d.qd + lq.astype(I32)
        same = iota((128, 128), 0) == lo.astype(I32)
        zero = jnp.zeros((128, 128), F32)
        right = jnp.concatenate(
            [
                jnp.concatenate([jnp.where(same & (hi > 0.0), 1.0, 0.0), zero], axis=1),
                jnp.concatenate([jnp.where(same, hi, 0.0), jnp.where(same, low, 0.0)], axis=1),
            ],
            axis=0,
        ).astype(BF16)
        step = max(1, 256 // d.grows)
        for c0 in range(0, d.blocks, step):
            left = hot(iota((step * d.grows, 128), 0) + c0 * d.grows == key)
            out = nt(jnp.concatenate([left, left], axis=1), right)
            rows = pl.ds(pl.multiple_of(g * d.grows, d.grows), d.grows)
            for k in range(step):
                cols = slice((c0 + k) * 128, (c0 + k + 1) * 128)
                nbuf[rows, cols] = out[k * d.grows : (k + 1) * d.grows, :128]
                tp = out[k * d.grows : (k + 1) * d.grows, 128:]
                tbuf[rows, cols] = tp
                et[pl.ds(pl.multiple_of(d.rows + g * d.grows, d.grows), d.grows), cols] = tp.astype(BF16)
        return 0

    lax.fori_loop(0, d.groups, fill, 0, unroll=min(8, d.groups))

    per = max(1, 16 // d.qd)
    for k in range(n):
        layer = lax.rem(z + k, n)
        count = d.layer - 1 if k == 0 else d.layer
        arrived(qrecv.at[pl.ds(layer * d.layer, count)], qr.at[layer])

        def place(i, _, layer=layer):
            first = layer * d.layer + i * per
            rows = [qrecv[first + j].astype(F32) for j in range(per)]
            at = pl.multiple_of(first * d.qd, per * d.qd)
            qall[pl.ds(at, per * d.qd)] = jnp.concatenate(rows, axis=0).astype(BF16)
            return 0

        lax.fori_loop(0, d.layer // per, place, 0, unroll=True)
        size = d.layer * d.qd
        here = pl.ds(pl.multiple_of(layer * size, size), size)
        there = pl.ds(pl.multiple_of(d.half + layer * size, size), size)
        send(qall.at[here], qall.at[there], xs.at[k], xr.at[layer], sibling)

    cache_copy.wait()
    cache_waited = True

    mbuf[...] = jnp.full(mbuf.shape, NEG, F32)
    zbuf[...] = jnp.zeros(zbuf.shape, F32)
    dbuf[...] = jnp.zeros(dbuf.shape, F32)
    halves = [slice(0, d.half), slice(d.half, d.rows)]
    tiles = [slice(t, t + d.tile) for t in range(0, d.held, d.tile)]
    step = min(64, d.half)

    def score(rows, cols):
        sbuf[rows, cols] = nt(qall[rows], c_ref[cols])

    def lanes(cols):
        return [slice(k, k + 128) for k in range(cols.start, cols.stop, 128)]

    def blocks(rows):
        return [slice(r, r + step) for r in range(rows.start, rows.stop, step)]

    def largest(rows, cols):
        for rr in blocks(rows):
            best, dot = mbuf[rr], dbuf[rr]
            for cc in lanes(cols):
                logits = sbuf[rr, cc] * scale
                dot = dot + tbuf[rr, cc] * logits
                best = jnp.maximum(best, jnp.where(nbuf[rr, cc] > 0.0, logits, NEG))
            mbuf[rr] = best
            dbuf[rr] = dot

    def widest(rows):
        mbuf[rows] = jnp.broadcast_to(jnp.max(mbuf[rows], axis=1, keepdims=True), (d.half, 128))

    def expo(rows, cols):
        for rr in blocks(rows):
            top, total = mbuf[rr], zbuf[rr]
            for cc in lanes(cols):
                e = nbuf[rr, cc] * jnp.exp(jnp.minimum(sbuf[rr, cc] * scale - top, 0.0))
                et[rr, cc] = e.astype(BF16)
                total = total + e
            zbuf[rr] = total

    for h in range(2):
        if h == 1:
            for layer in range(n):
                size = d.layer * d.qd
                arrived(qall.at[pl.ds(d.half + layer * size, size)], xr.at[layer])
        for cols in tiles:
            score(halves[h], cols)
        for cols in tiles:
            largest(halves[h], cols)
        widest(halves[h])
        for cols in tiles:
            expo(halves[h], cols)

    nr = d.stat_rows
    my_top = col_to_rows(mbuf[:, :1])
    packed = [
        my_top,
        col_to_rows(jnp.sum(zbuf[...], axis=1, keepdims=True)),
        col_to_rows(jnp.sum(dbuf[...], axis=1, keepdims=True)),
    ]
    spare = [jnp.zeros((16 - 3 * nr, 128), F32)] if 16 - 3 * nr else []
    stat[...] = jnp.concatenate(packed + spare, axis=0)

    def swap(v):
        return jnp.concatenate([v[nr // 2 :], v[: nr // 2]], axis=0)

    def combine(pieces):
        tops = [p[0] for p in pieces]
        best = functools.reduce(jnp.maximum, tops)
        zs = sum(p[1] * jnp.exp(t - best) for p, t in zip(pieces, tops))
        ds = sum(p[2] for p in pieces)
        return best, zs, ds

    def three(v):
        return [v[:nr], v[nr : 2 * nr], v[2 * nr : 3 * nr]]

    for k in far_xc:
        send(stat, sa.at[k], sas.at[k], sar.at[k], dev_xc(lax.rem(xc + k, nxc)))

    def product(rows):
        uv[rows] = nn(et[rows], c_ref[...])

    product(slice(0, d.rows))
    for k in range(1, nxc):
        arrived(sa.at[k], sar.at[k])
    pieces = [three(stat[...])]
    for k in range(1, nxc):
        got = three(sa[k])
        pieces.append([swap(v) for v in got] if k % 2 else got)
    stat2[...] = jnp.concatenate(list(combine(pieces)) + spare, axis=0)
    for k in far_yz:
        send(stat2, sb.at[k], sbs.at[k], sbr.at[k], dev_yz(lax.rem(yz + k, nyz)))
    product(slice(d.rows, 2 * d.rows))
    for k in range(1, nyz):
        arrived(sb.at[k], sbr.at[k])
    best, zs, ds = combine([three(stat2[...])] + [three(sb[k]) for k in range(1, nyz)])

    zbuf[...] = jnp.broadcast_to(rows_to_col(scale * jnp.exp(my_top - best) / zs), zbuf.shape)

    def part(rows, cols):
        wide = jnp.concatenate([zbuf[rows]] * (d.cut // 128), axis=1)
        return uv[rows, cols] * wide - uv[slice(d.rows + rows.start, d.rows + rows.stop), cols] * scale

    cuts = [slice(i * d.cut, (i + 1) * d.cut) for i in range(CUTS)]
    for i in range(CUTS):
        csend[i] = part(halves[1], cuts[i]).astype(BF16)
        send(csend.at[i], crecv.at[i], cs.at[i], cr.at[i], sibling)

    for i in range(CUTS):
        mine = part(halves[0], cuts[i])
        arrived(crecv.at[i], cr.at[i])
        uv[halves[0], cuts[i]] = mine + crecv[i].astype(F32)
        size = max(8, d.qd)

        def split(j, _, i=i):
            rows = uv[pl.ds(pl.multiple_of(j * size, size), size), cuts[i]]
            for k in range(size // d.qd):
                psend[i, j * (size // d.qd) + k] = rows[k * d.qd : (k + 1) * d.qd].astype(BF16)
            return 0

        lax.fori_loop(0, d.half // size, split, 0, unroll=4)
        precv[i, chip] = psend[i, chip]

        def give_back(k, _, i=i):
            to, h = other(k)
            remote(psend.at[i, h], precv.at[i, chip], ps.at[i], pr.at[i], to).start()
            return 0

        lax.fori_loop(0, d.chips - 1, give_back, 0, unroll=3)

    losses = best + jnp.log(zs) - ds
    flat = iota((nr, 128), 0) * 128 + iota((nr, 128), 1)
    out = jnp.zeros((1, 128), F32)
    for i in range(d.qd):
        value = jnp.sum(
            jnp.sum(jnp.where(flat == chip * d.qd + i, losses, 0.0), axis=0, keepdims=True),
            axis=1,
            keepdims=True,
        )
        out = jnp.where(iota((1, 128), 1) == i, value + entropy[i : i + 1], out)
    loss_ref[...] = out[:, : d.qd]

    for i in range(CUTS):
        arrived(precv.at[i, pl.ds(0, d.chips - 1)], pr.at[i])
        grad_ref[:, cuts[i]] = lax.fori_loop(
            0,
            d.chips,
            lambda h, total, i=i: total + precv[i, h].astype(F32),
            jnp.zeros((d.qd, d.cut), F32),
            unroll=8,
        )

    for copy in pending:
        copy.wait_send()
    sent(qrecv.at[pl.ds(0, d.chips - 1)], qs.at[0])
    sent(ra.at[pl.ds(0, d.chips - 1)], tas.at[0])
    for i in range(CUTS):
        sent(psend.at[i, pl.ds(0, d.chips - 1)], ps.at[i])


def hand_over(grad_ref, loss_ref, grad_out, loss_out):
    grad_out[...] = grad_ref[...]
    loss_out[...] = loss_ref[...]


def per_device(n, queries, cache, cand_ids, owner_map, teacher_rank):
    d = Dims(n, queries.shape, cache.shape, cand_ids.shape)
    w = d.width
    nxc, nyz = 2 * n, n * n
    dma = lambda k: [pltpu.SemaphoreType.DMA((k,))] * 2
    vmem = pl.BlockSpec(memory_space=pltpu.VMEM)
    grad, loss = pl.pallas_call(
        functools.partial(kernel, d),
        out_shape=(
            jax.ShapeDtypeStruct((d.qd, w), F32),
            jax.ShapeDtypeStruct((1, d.qd), F32),
        ),
        in_specs=[pl.BlockSpec(memory_space=pl.ANY)] * 5,
        out_specs=(vmem, vmem),
        scratch_shapes=[
            pltpu.VMEM((d.qd, w), F32),
            pltpu.VMEM((d.qd, d.cands), I32),
            pltpu.VMEM((owner_map.shape[0] // 128, 128), I32),
            pltpu.VMEM((d.qd, d.cands), I32),
            pltpu.VMEM((d.held, w), BF16),
            pltpu.VMEM((d.qd, w), BF16),
            pltpu.VMEM((d.chips, d.qd, w), BF16),
            pltpu.VMEM((d.rows, w), BF16),
            pltpu.VMEM((d.chips, 2, 128), F32),
            pltpu.VMEM((d.chips, 2, 128), F32),
            pltpu.VMEM((d.chips, 128), F32),
            pltpu.VMEM((d.devices, 128), F32),
            pltpu.VMEM((5, d.groups, 128), F32),
            pltpu.VMEM((d.rows, d.held), F32),
            pltpu.VMEM((d.rows, d.held), F32),
            pltpu.VMEM((d.rows, d.held), F32),
            pltpu.VMEM((2 * d.rows, d.held), BF16),
            pltpu.VMEM((d.rows, 128), F32),
            pltpu.VMEM((d.rows, 128), F32),
            pltpu.VMEM((d.rows, 128), F32),
            pltpu.VMEM((16, 128), F32),
            pltpu.VMEM((nxc, 16, 128), F32),
            pltpu.VMEM((16, 128), F32),
            pltpu.VMEM((nyz, 16, 128), F32),
            pltpu.VMEM((2 * d.rows, w), F32),
            pltpu.VMEM((CUTS, d.half, d.cut), BF16),
            pltpu.VMEM((CUTS, d.half, d.cut), BF16),
            pltpu.VMEM((CUTS, d.chips, d.qd, d.cut), BF16),
            pltpu.VMEM((CUTS, d.chips, d.qd, d.cut), BF16),
            pltpu.SemaphoreType.DMA((4,)),
            pltpu.SemaphoreType.DMA,
            pltpu.SemaphoreType.DMA((1,)),
            pltpu.SemaphoreType.DMA((n,)),
            *dma(n),
            *dma(1),
            *dma(1),
            *dma(nxc),
            *dma(nyz),
            *dma(CUTS),
            *dma(CUTS),
        ],
        compiler_params=pltpu.CompilerParams(
            collective_id=0, has_side_effects=True, vmem_limit_bytes=60 * 2**20
        ),
    )(queries, cand_ids, owner_map.reshape(-1, 128), teacher_rank, cache)
    grad, loss = pl.pallas_call(
        hand_over,
        out_shape=(
            jax.ShapeDtypeStruct((d.qd, w), F32),
            jax.ShapeDtypeStruct((1, d.qd), F32),
        ),
        in_specs=[vmem] * 2,
        out_specs=(vmem, vmem),
    )(grad, loss)
    return grad, loss.reshape(d.qd)


def solution(mesh):
    n = mesh.shape["grp"]
    both = P(("grp", "shard"), None)
    return jax.shard_map(
        functools.partial(per_device, n),
        mesh=mesh,
        in_specs=(both, both, both, P(), both),
        out_specs=(both, P(("grp", "shard"))),
        check_vma=False,
    )
```
